512 devices in a mesh: dp: 32 (over z, y_hi), mp: 16 (over y_lo, x, core).
Axes of the slice: x: 4, y: 8 (y_hi: 4, y_lo: 2; y = y_hi * 2 + y_lo), z: 8, core: 2. Of those that a mesh axis runs over, the one named last changes fastest.
Arguments:
- attention: bfloat16 [4096, 8192], P('dp', 'mp'), may hold values from -6 to 6
- output_projection: bfloat16 [8192, 8192], P('mp', 'dp'), may hold values from -0.0625 to 0.0625
- residual: bfloat16 [4096, 8192], P('dp', 'mp'), may hold values from -6 to 6
- final_norm_gain: bfloat16 [8192], P('mp'), may hold values from 0.099609375 to 1.8984375
- draft_projection_weight: bfloat16 [8192, 4096], P(None, 'mp'), may hold values from -0.0625 to 0.0625
- adapter_down_weight: bfloat16 [8192, 512], P('mp', 'dp'), may hold values from -0.0625 to 0.0625
- adapter_up_weight: bfloat16 [4096, 512], P('mp', 'dp'), may hold values from -1.5 to 1.5
- token_tenant_index: int32 [4096], P('dp'), may hold values from 0 to 31, as said below
- tenant_token_count: int32 [32], replicated, may hold values from 32 to 511
Outputs:
- grad_down: float32 [8192, 512], P('mp', 'dp')
- grad_up: float32 [4096, 512], P('mp', 'dp')
The draws below stay inside these ranges and needn't reach their ends.
Inputs may be any that keep to these rules, and one draw needn't show every extreme that they name: `token_tenant_index`: tokens come in runs of one tenant; every tenant has tokens.
All inputs are finite; a program needn't handle non-finite values.
Results may differ from the reference program's by a relative error of at most 0.03.
Values may be sent and summed in bfloat16 or wider, within the bound.
No kernel may reach another device: no remote copies, remote signals or barrier semaphores. Data moves between devices by JAX's collectives and lax.ppermute only.
A program may use at most 64 MiB of HBM per device.

```python
import jax
import jax.numpy as jnp
from jax import lax

MODEL_WIDTH = 8192
HQ = 8192
DRAFT_WIDTH = 4096
TENANT_COUNT = 32
ADAPTER_RANK = 16
TOK_DEV = 128
TOKENS = 4096
N_MP = 16


def draw_token_tenant_index(key, part):
    key = jax.random.fold_in(key, 7)
    key_starts, key_first, key_second, key_order = jax.random.split(key, 4)
    period = max(1, TOKENS // (2 * TENANT_COUNT))
    position = jnp.arange(TOKENS, dtype=jnp.int32)
    starts = (jax.random.randint(key_starts, (TOKENS,), 0, 16) == 0) | (position % period == 0)
    segment = jnp.cumsum(starts.astype(jnp.int32)) - 1
    first_draw = jax.random.randint(key_first, (TOKENS,), 0, TENANT_COUNT)
    second_draw = jax.random.randint(key_second, (TOKENS,), 0, TENANT_COUNT)
    tenant_order = jax.random.permutation(key_order, TENANT_COUNT).astype(jnp.int32)
    segment_tenant = tenant_order[jnp.minimum(first_draw, second_draw)]
    segment_tenant = segment_tenant.at[:TENANT_COUNT].set(tenant_order)
    return segment_tenant[segment].astype(jnp.int32)


def place_ends(array, stream_key, low, largest):
    spot = [jax.random.randint(jax.random.fold_in(stream_key, axis), (), 0, length) for axis, length in enumerate(array.shape)]
    main_axis = array.shape.index(max(array.shape))
    beside = spot[:main_axis] + [(spot[main_axis] + 1) % array.shape[main_axis]] + spot[main_axis + 1:]
    return array.at[tuple(spot)].set(low).at[tuple(beside)].set(largest)


def levels(key, extent, cuts, least, largest):
    def one(dim, blocks):
        heights = jax.random.uniform(jax.random.fold_in(jax.random.fold_in(key, 6), dim), (blocks,), jnp.float32, least / len(cuts), largest / len(cuts))
        return jnp.repeat(jnp.exp(heights), extent[dim] // blocks).reshape((-1,) + (1,) * (len(extent) - dim - 1))

    gain = one(*cuts[0])
    for cut in cuts[1:]:
        gain = gain * one(*cut)
    return gain


def centred(rng, shape, scale, limit, cuts=(), kind=jnp.bfloat16):
    factor_of = levels(rng, shape, cuts, -0.22, 0.18) if cuts else 1.0
    drawn = jax.random.normal(rng, shape, jnp.float32) * scale * factor_of
    return jnp.minimum(jnp.maximum(drawn, -limit), limit).astype(kind)


def setup_inputs(seed: int = 0) -> dict:
    seeds = jax.random.split(jax.random.key(seed), 10)
    return {
        "attention": centred(seeds[0], (TOKENS, HQ), 1.0, 6.0, ((0, 32), (1, 16))),
        "output_projection": centred(seeds[1], (HQ, MODEL_WIDTH), HQ ** -0.5, 0.0625, ((0, 16), (1, 32))),
        "residual": centred(seeds[2], (TOKENS, MODEL_WIDTH), 1.0, 6.0, ((0, 32), (1, 16))),
        "final_norm_gain": jnp.clip(1.0 + 0.18 * jax.random.normal(seeds[3], (MODEL_WIDTH,), jnp.float32), 0.099609375, 1.8984375).astype(jnp.bfloat16),
        "draft_projection_weight": centred(seeds[4], (MODEL_WIDTH, DRAFT_WIDTH), MODEL_WIDTH ** -0.5, 0.0625, ((1, 16),)),
        "adapter_down_weight": centred(seeds[5], (MODEL_WIDTH, TENANT_COUNT * ADAPTER_RANK), MODEL_WIDTH ** -0.5, 0.0625, ((0, 16), (1, 32))),
        "adapter_up_weight": centred(seeds[6], (DRAFT_WIDTH, TENANT_COUNT * ADAPTER_RANK), ADAPTER_RANK ** -0.5, 1.5, ((0, 16), (1, 32))),
        "token_tenant_index": draw_token_tenant_index(jax.random.fold_in(seeds[9], 71), 0),
        "tenant_token_count": place_ends(jax.random.randint(seeds[8], (TENANT_COUNT,), 32, 512), jax.random.fold_in(seeds[8], 1), 32, 511).astype(jnp.int32),
    }


EPSILON = 1e-06
ADAPTER_SCALE = 2.0
TOP_PRECISION = lax.Precision.HIGHEST

def select_tenant(values, tenant_indicator):
    spread = values.reshape(values.shape[0], TENANT_COUNT, ADAPTER_RANK)
    return lax.optimization_barrier(jnp.sum(spread * tenant_indicator[:, :, None].astype(jnp.float32), axis=1))

def widen(values, tenant_indicator):
    return jnp.tile(values, (1, TENANT_COUNT)) * jnp.repeat(tenant_indicator, ADAPTER_RANK, axis=1)

def reference(attention, output_projection, residual, final_norm_gain, draft_projection_weight, adapter_down_weight, adapter_up_weight, token_tenant_index, tenant_token_count):
    head_block = HQ // N_MP

    def add_block(block_index, total_sum):
        first_row = jnp.asarray(block_index).astype(jnp.int32) * head_block
        head_rows = lax.dynamic_slice_in_dim(attention, first_row, head_block, 1)
        weights = lax.dynamic_slice_in_dim(output_projection, first_row, head_block, 0)
        block_term = jnp.dot(head_rows, weights, preferred_element_type=jnp.float32).astype(jnp.bfloat16)
        block_term = lax.optimization_barrier(block_term)
        return total_sum + block_term.astype(jnp.float32)
    projected = lax.fori_loop(0, N_MP, add_block, jnp.zeros((TOKENS, MODEL_WIDTH), jnp.float32))
    hidden = residual.astype(jnp.float32) + projected
    inv_rms = lax.rsqrt(lax.optimization_barrier(jnp.mean(hidden * hidden, axis=1)) + EPSILON)
    normalized_features = hidden * final_norm_gain.astype(jnp.float32)[None, :] * inv_rms[:, None]
    verifier_features = normalized_features.astype(jnp.bfloat16)
    tenant_indicator = (token_tenant_index[:, None] == jnp.arange(TENANT_COUNT, dtype=jnp.int32)[None, :]).astype(jnp.float32)
    onehot_half = tenant_indicator.astype(jnp.bfloat16)
    down_every_tenant = jnp.dot(normalized_features, adapter_down_weight.astype(jnp.float32), precision=TOP_PRECISION)
    low_codes = select_tenant(down_every_tenant, tenant_indicator)
    low_rank_widened = widen(low_codes.astype(jnp.bfloat16), onehot_half)
    adapter_change = jnp.dot(low_rank_widened, adapter_up_weight.T, preferred_element_type=jnp.float32)
    draft_output = jnp.dot(verifier_features, draft_projection_weight, preferred_element_type=jnp.float32) + ADAPTER_SCALE * adapter_change
    target = jnp.roll(verifier_features[:, :DRAFT_WIDTH], -1, axis=0).astype(jnp.float32)
    position = jnp.arange(TOKENS, dtype=jnp.int32) % TOK_DEV
    keep_mask = (position < TOK_DEV - 1) & (token_tenant_index == jnp.roll(token_tenant_index, -1))
    weight = keep_mask.astype(jnp.float32) / jnp.dot(tenant_indicator, tenant_token_count.astype(jnp.float32), precision=TOP_PRECISION)
    grad_draft = (draft_output - target) * weight[:, None]
    gradient_rounded = grad_draft.astype(jnp.bfloat16)
    backward_low_rank = ADAPTER_SCALE * select_tenant(jnp.dot(gradient_rounded, adapter_up_weight, preferred_element_type=jnp.float32), tenant_indicator)
    back_round = backward_low_rank.astype(jnp.bfloat16)
    grad_up = jnp.dot(gradient_rounded.T, low_rank_widened, preferred_element_type=jnp.float32)
    grad_down = jnp.dot(verifier_features.T, widen(back_round, onehot_half), preferred_element_type=jnp.float32)
    return (grad_down, grad_up)
```

```python
import jax
import jax.numpy as jnp
from jax import lax
from jax.sharding import Mesh
from jax.sharding import PartitionSpec as P

EPSILON = 1e-06
ADAPTER_SCALE = 2.0
BF = jnp.bfloat16
F32 = jnp.float32

AXES = ("z", "yh", "yl", "x", "c")
SIZES = (8, 4, 2, 4, 2)
DP = ("z", "yh")
MP = ("yl", "x", "c")
CHIPS = ("yl", "x")


def dot(subscripts, left, right):
    return jnp.einsum(subscripts, left, right, preferred_element_type=F32)


def swap(value):
    return lax.ppermute(value, "c", [(0, 1), (1, 0)])


def exchange(value, axis):
    return lax.all_to_all(value, axis, 0, 0)


def gather(value, axis, size):
    return exchange(jnp.broadcast_to(value[None], (size,) + value.shape), axis)


def split(value):
    high = value.astype(BF)
    return high, (value - high.astype(F32)).astype(BF)


def half(value, which, length, axis=0):
    return lax.dynamic_slice_in_dim(value, which * length, length, axis)


def shards(attention, output_projection, residual, gain, draft_weight, down, up, tenant_of, tenant_count):
    n_z, n_yh, n_yl, n_x, _ = SIZES
    n_chips = n_yl * n_x
    tenants = tenant_count.shape[0]
    rank = down.shape[1]
    tokens, block = residual.shape
    cols = output_projection.shape[1]
    out_block = draft_weight.shape[1]
    width = block * 2 * n_chips
    mine = tokens // 2
    core = lax.axis_index("c")
    chip = lax.axis_index(CHIPS)
    other = 1 - core
    first = core == 0

    def ordered(own, others):
        return jnp.where(first, own, others), jnp.where(first, others, own)

    proj = lax.all_gather(output_projection, "z", axis=0)
    draft_weight_other = swap(draft_weight)
    pad = jnp.broadcast_to(gain[None], (16, block))
    kept = swap(jnp.concatenate([half(residual, other, mine), pad], axis=0))
    residual_parts = ordered(half(residual, core, mine), kept[:mine])
    gain_parts = ordered(gain[None], kept[mine : mine + 1])

    adapters = jnp.concatenate([down.T, up.T], axis=1)
    adapters = gather(adapters, "z", n_z).reshape(n_z * rank, block + out_block)
    joined = gather(jnp.concatenate([attention, adapters], axis=1), "yh", n_yh)
    attention_all = joined[:, :, :block]
    adapters_all = joined[:, :, block:].reshape(tenants * rank, block + out_block)
    adapters_other = swap(adapters_all)
    down_parts = ordered(adapters_all[:, :block], adapters_other[:, :block])
    up_own, up_other = adapters_all[:, block:], adapters_other[:, block:]

    rows = n_yh * mine
    send = half(attention_all, other, mine, 1).reshape(rows, block)
    keep = half(attention_all, core, mine, 1).reshape(rows, block)
    sent = swap(dot("tk,zkn->ztn", send, proj).astype(BF))
    pair = (dot("tk,zkn->ztn", keep, proj) + sent.astype(F32)).astype(BF)
    summed = jnp.sum(exchange(pair, CHIPS).astype(F32), axis=0).astype(BF)
    projected = exchange(summed.reshape(n_yh, mine, cols), "yh")

    half_yh = n_yh // 2
    scaled, squares = [], 0.0
    for part in range(2):
        piece = jnp.concatenate(
            [projected[half_yh * part + j] for j in range(half_yh)], axis=1
        ).astype(F32)
        hidden = residual_parts[part].astype(F32) + piece
        squares = squares + jnp.sum(hidden * hidden, axis=1, keepdims=True)
        scaled.append((hidden * gain_parts[part].astype(F32)).astype(BF))
    own_scaled = jnp.where(first, scaled[0], scaled[1])
    partner_scaled = swap(jnp.where(first, scaled[1], scaled[0]))

    slot = jnp.arange(tenants * rank, dtype=jnp.int32) // rank
    slot_tenant = (slot % n_z) * n_yh + slot // n_z
    own_tenant = half(tenant_of, core, mine)
    partner_tenant = half(tenant_of, other, mine)
    own_mask = slot_tenant[:, None] == own_tenant[None, :]
    partner_mask = slot_tenant[:, None] == partner_tenant[None, :]

    def select(values):
        chosen = jnp.where(own_mask, values, 0.0)
        return jnp.sum(chosen.reshape(tenants, rank, mine), axis=0)

    def widen(values, mask):
        return jnp.where(mask, jnp.tile(values, (tenants, 1)), BF(0))

    low_part = select(dot("jd,td->jt", down_parts[0], scaled[0]) + dot("jd,td->jt", down_parts[1], scaled[1]))
    extras = jnp.concatenate(split(low_part), axis=0).T
    message = jnp.concatenate(
        scaled + [extras, *split(squares), jnp.zeros((mine, 128 - 2 * rank - 2), BF)], axis=1
    )
    received = gather(message, CHIPS, n_chips)
    features = received[:, :, : 2 * block]
    totals = jnp.sum(received[:, :, 2 * block :].astype(F32), axis=0)
    square_column = totals[:, 2 * rank : 2 * rank + 1] + totals[:, 2 * rank + 1 : 2 * rank + 2]
    inv_column = lax.rsqrt(square_column / width + EPSILON)
    totals = totals.T
    inv_row = lax.rsqrt((totals[2 * rank : 2 * rank + 1] + totals[2 * rank + 1 : 2 * rank + 2]) / width + EPSILON)
    low_round = ((totals[:rank] + totals[rank : 2 * rank]) * inv_row).astype(BF)
    low_wide = widen(low_round, own_mask)

    target = lax.dynamic_slice(
        features, (chip // 2, 0, (chip % 2) * 2 * out_block), (1, mine, 2 * out_block)
    )[0]
    target = (target.astype(F32) * inv_column).astype(BF)
    next_row = swap(target[:16])[:1]
    target = jnp.concatenate([target[1:], next_row], axis=0)
    target_own = half(target, core, out_block, 1).astype(F32)
    target_other = half(target, other, out_block, 1).astype(F32)

    following = jnp.roll(tenant_of, -1)
    position = jnp.arange(tokens, dtype=jnp.int32)
    keep_mask = (position < tokens - 1) & (tenant_of == following)
    is_tenant = tenant_of[:, None] == jnp.arange(tenants, dtype=jnp.int32)[None, :]
    count = jnp.sum(jnp.where(is_tenant, tenant_count.astype(F32)[None, :], 0.0), axis=1)
    weight = half(keep_mask.astype(F32) / count, core, mine)[:, None]

    def draft(weights, ups):
        shaped = weights.reshape(n_chips, 2 * block, out_block)
        return dot("ktd,kdn->tn", features, shaped) * inv_column + ADAPTER_SCALE * dot("jt,jn->tn", low_wide, ups)

    grad_other = ((draft(draft_weight_other, up_other) - target_other) * weight).astype(BF)
    low_lanes = jnp.concatenate([low_round.T, jnp.zeros((mine, 128 - rank), BF)], axis=1)
    partner = swap(jnp.concatenate([grad_other, low_lanes], axis=1))
    grad_own = ((draft(draft_weight, up_own) - target_own) * weight).astype(BF)

    back_part = select(dot("jc,tc->jt", up_own, grad_own) + dot("jc,tc->jt", up_other, grad_other))
    back = jnp.sum(gather(back_part, CHIPS, n_chips), axis=0)
    back_scaled = (ADAPTER_SCALE * back * inv_row).astype(BF)
    back_partner = swap(back_scaled)

    grad_up = dot("jt,tc->jc", low_wide, grad_own) + dot(
        "jt,tc->jc", widen(partner[:, out_block : out_block + rank].T, partner_mask), partner[:, :out_block]
    )
    grad_down = dot("jt,td->jd", widen(back_scaled, own_mask), own_scaled) + dot(
        "jt,td->jd", widen(back_partner, partner_mask), partner_scaled
    )
    grads = jnp.concatenate([grad_down.astype(BF), grad_up.astype(BF)], axis=1)
    grads = exchange(grads.reshape(n_yh, n_z * rank, block + out_block), "yh")
    grads = jnp.sum(grads.astype(F32), axis=0).astype(BF)
    grads = exchange(grads.reshape(n_z, rank, block + out_block), "z")
    grads = jnp.sum(grads.astype(F32), axis=0)
    return grads[:, :block].T, grads[:, block:].T


def solution(mesh):
    split_mesh = Mesh(mesh.devices.reshape(SIZES), AXES)
    return jax.shard_map(
        shards,
        mesh=split_mesh,
        in_specs=(
            P(DP, MP),
            P(MP, DP),
            P(DP, MP),
            P(MP),
            P(None, MP),
            P(MP, DP),
            P(MP, DP),
            P(DP),
            P(),
        ),
        out_specs=(P(MP, DP), P(MP, DP)),
        check_vma=False,
    )
```

```python
import jax
import jax.numpy as jnp
from jax import lax
from jax.sharding import Mesh
from jax.sharding import PartitionSpec as P

EPSILON = 1e-06
ADAPTER_SCALE = 2.0
BF = jnp.bfloat16
F32 = jnp.float32

AXES = ("z", "yh", "yl", "x", "c")
SIZES = (8, 4, 2, 4, 2)
DP = ("z", "yh")
MP = ("yl", "x", "c")
CHIPS = ("yl", "x")


def dot(subscripts, left, right):
    return jnp.einsum(subscripts, left, right, preferred_element_type=F32)


def swap(value):
    return lax.ppermute(value, "c", [(0, 1), (1, 0)])


def exchange(value, axis):
    return lax.all_to_all(value, axis, 0, 0)


def gather(value, axis, size):
    return exchange(jnp.broadcast_to(value[None], (size,) + value.shape), axis)


def split(value):
    high = value.astype(BF)
    return high, (value - high.astype(F32)).astype(BF)


def half(value, which, length, axis=0):
    return lax.dynamic_slice_in_dim(value, which * length, length, axis)


def shards(attention, output_projection, residual, gain, draft_weight, down, up, tenant_of, tenant_count):
    n_z, n_yh, n_yl, n_x, _ = SIZES
    n_chips = n_yl * n_x
    tenants = tenant_count.shape[0]
    rank = down.shape[1]
    tokens, block = residual.shape
    cols = output_projection.shape[1]
    out_block = draft_weight.shape[1]
    width = block * 2 * n_chips
    mine = tokens // 2
    core = lax.axis_index("c")
    chip = lax.axis_index(CHIPS)
    other = 1 - core
    first = core == 0

    def ordered(own, others):
        return jnp.where(first, own, others), jnp.where(first, others, own)

    proj = lax.all_gather(output_projection, "z", axis=0)
    draft_weight_other = swap(draft_weight)
    pad = jnp.broadcast_to(gain[None], (16, block))
    kept = swap(jnp.concatenate([half(residual, other, mine), pad], axis=0))
    residual_parts = ordered(half(residual, core, mine), kept[:mine])
    gain_parts = ordered(gain[None], kept[mine : mine + 1])

    adapters = jnp.concatenate([down.T, up.T], axis=1)
    adapters_kept = swap(adapters)
    packed = [
        *ordered(adapters[:, :block], adapters_kept[:, :block]),
        jnp.concatenate([adapters[:, block:], adapters_kept[:, block:]], axis=1),
    ]
    joined = gather(jnp.concatenate([attention, *packed], axis=0), "yh", n_yh)
    attention_all = joined[:, :tokens]
    adapters_yh, proj = lax.optimization_barrier((joined[:, tokens:], proj))
    adapters_all = lax.all_gather(adapters_yh.reshape(n_yh * 3 * rank, block), "z", axis=0)
    adapters_all = adapters_all.reshape(tenants, 3, rank, block)
    down_parts = [adapters_all[:, part].reshape(tenants * rank, block) for part in range(2)]
    ups = adapters_all[:, 2].reshape(tenants * rank, 2 * out_block)

    rows = n_yh * mine
    send = half(attention_all, other, mine, 1).reshape(rows, block)
    keep = half(attention_all, core, mine, 1).reshape(rows, block)
    sent = swap(dot("tk,zkn->ztn", send, proj).astype(BF))
    pair = (dot("tk,zkn->ztn", keep, proj) + sent.astype(F32)).astype(BF)
    summed = jnp.sum(exchange(pair, CHIPS).astype(F32), axis=0).astype(BF)
    projected = exchange(summed.reshape(n_yh, mine, cols), "yh")

    half_yh = n_yh // 2
    scaled, squares = [], 0.0
    for part in range(2):
        piece = jnp.concatenate(
            [projected[half_yh * part + j] for j in range(half_yh)], axis=1
        ).astype(F32)
        hidden = residual_parts[part].astype(F32) + piece
        squares = squares + jnp.sum(hidden * hidden, axis=1, keepdims=True)
        scaled.append((hidden * gain_parts[part].astype(F32)).astype(BF))
    own_scaled = jnp.where(first, scaled[0], scaled[1])
    partner_scaled = swap(jnp.where(first, scaled[1], scaled[0]))

    slot_tenant = jnp.arange(tenants * rank, dtype=jnp.int32) // rank
    own_tenant = half(tenant_of, core, mine)
    partner_tenant = half(tenant_of, other, mine)
    own_mask = slot_tenant[:, None] == own_tenant[None, :]
    partner_mask = slot_tenant[:, None] == partner_tenant[None, :]

    def select(values):
        chosen = jnp.where(own_mask, values, 0.0)
        return jnp.sum(chosen.reshape(tenants, rank, mine), axis=0)

    def widen(values, mask):
        return jnp.where(mask, jnp.tile(values, (tenants, 1)), BF(0))

    low_part = select(dot("jd,td->jt", down_parts[0], scaled[0]) + dot("jd,td->jt", down_parts[1], scaled[1]))
    extras = jnp.concatenate(split(low_part), axis=0).T
    message = jnp.concatenate(
        scaled + [extras, *split(squares), jnp.zeros((mine, 128 - 2 * rank - 2), BF)], axis=1
    )
    received = gather(message, CHIPS, n_chips)
    features = received[:, :, : 2 * block]
    totals = jnp.sum(received[:, :, 2 * block :].astype(F32), axis=0)
    square_column = totals[:, 2 * rank : 2 * rank + 1] + totals[:, 2 * rank + 1 : 2 * rank + 2]
    inv_column = lax.rsqrt(square_column / width + EPSILON)
    totals = totals.T
    inv_row = lax.rsqrt((totals[2 * rank : 2 * rank + 1] + totals[2 * rank + 1 : 2 * rank + 2]) / width + EPSILON)
    low_round = ((totals[:rank] + totals[rank : 2 * rank]) * inv_row).astype(BF)
    low_wide = widen(low_round, own_mask)

    target = lax.dynamic_slice(
        features, (chip // 2, 0, (chip % 2) * 2 * out_block), (1, mine, 2 * out_block)
    )[0]
    target = (target.astype(F32) * inv_column).astype(BF)
    next_row = swap(target[:16])[:1]
    target = jnp.concatenate([target[1:], next_row], axis=0)
    target = jnp.concatenate([half(target, core, out_block, 1), half(target, other, out_block, 1)], axis=1)

    following = jnp.roll(tenant_of, -1)
    position = jnp.arange(tokens, dtype=jnp.int32)
    keep_mask = (position < tokens - 1) & (tenant_of == following)
    is_tenant = tenant_of[:, None] == jnp.arange(tenants, dtype=jnp.int32)[None, :]
    count = jnp.sum(jnp.where(is_tenant, tenant_count.astype(F32)[None, :], 0.0), axis=1)
    weight = half(keep_mask.astype(F32) / count, core, mine)[:, None]

    both_weights = jnp.concatenate([draft_weight, draft_weight_other], axis=1)
    draft = dot("ktd,kdn->tn", features, both_weights.reshape(n_chips, 2 * block, 2 * out_block)) * inv_column
    draft = draft + ADAPTER_SCALE * dot("jt,jn->tn", low_wide, ups)
    grad = ((draft - target.astype(F32)) * weight).astype(BF)
    grad_own = grad[:, :out_block]

    back_part = select(dot("jc,tc->jt", ups, grad))
    low_lanes = jnp.concatenate([low_round.T, *split(inv_column), jnp.zeros((mine, 126 - rank), BF)], axis=1)
    partner = jnp.concatenate([grad[:, out_block:], low_lanes], axis=1)
    back_part, partner = lax.optimization_barrier((back_part, partner))
    backs = gather(back_part, MP, 2 * n_chips)
    partner = swap(partner)
    backs = jnp.sum(backs.reshape(n_chips, 2, rank, mine), axis=0)
    partner_codes = partner[:, out_block:].T
    inv_partner = partner_codes[rank : rank + 1].astype(F32) + partner_codes[rank + 1 : rank + 2].astype(F32)
    back_scaled = (ADAPTER_SCALE * half(backs, core, 1)[0] * inv_row).astype(BF)
    back_partner = (ADAPTER_SCALE * half(backs, other, 1)[0] * inv_partner).astype(BF)

    grad_up = dot("jt,tc->jc", low_wide, grad_own) + dot(
        "jt,tc->jc", widen(partner_codes[:rank], partner_mask), partner[:, :out_block]
    )
    grad_down = dot("jt,td->jd", widen(back_scaled, own_mask), own_scaled) + dot(
        "jt,td->jd", widen(back_partner, partner_mask), partner_scaled
    )
    grads = jnp.concatenate([grad_down.astype(BF), grad_up.astype(BF)], axis=1)
    grads = exchange(grads.reshape(tenants, rank, block + out_block), DP)
    grads = jnp.sum(grads.astype(F32), axis=0)
    return grads[:, :block].T, grads[:, block:].T


def solution(mesh):
    split_mesh = Mesh(mesh.devices.reshape(SIZES), AXES)
    return jax.shard_map(
        shards,
        mesh=split_mesh,
        in_specs=(
            P(DP, MP),
            P(MP, DP),
            P(DP, MP),
            P(MP),
            P(None, MP),
            P(MP, DP),
            P(MP, DP),
            P(DP),
            P(),
        ),
        out_specs=(P(MP, DP), P(MP, DP)),
        check_vma=False,
    )
```

```python
import jax
import jax.numpy as jnp
from jax import lax
from jax.sharding import Mesh
from jax.sharding import PartitionSpec as P

EPSILON = 1e-06
ADAPTER_SCALE = 2.0
BF = jnp.bfloat16
F32 = jnp.float32

AXES = ("z", "yh", "yl", "x", "c")
SIZES = (8, 4, 2, 4, 2)
DP = ("z", "yh")
MP = ("yl", "x", "c")
CHIPS = ("yl", "x")


def dot(subscripts, left, right):
    return jnp.einsum(subscripts, left, right, preferred_element_type=F32)


def swap(value):
    return lax.ppermute(value, "c", [(0, 1), (1, 0)])


def exchange(value, axis):
    return lax.all_to_all(value, axis, 0, 0)


def gather(value, axis, size):
    return exchange(jnp.broadcast_to(value[None], (size,) + value.shape), axis)


def split(value):
    high = value.astype(BF)
    return high, (value - high.astype(F32)).astype(BF)


def half(value, which, length, axis=0):
    return lax.dynamic_slice_in_dim(value, which * length, length, axis)


def shards(attention, output_projection, residual, gain, draft_weight, down, up, tenant_of, tenant_count):
    n_z, n_yh, n_yl, n_x, _ = SIZES
    n_chips = n_yl * n_x
    tenants = tenant_count.shape[0]
    rank = down.shape[1]
    tokens, block = residual.shape
    cols = output_projection.shape[1]
    out_block = draft_weight.shape[1]
    width = block * 2 * n_chips
    mine = tokens // 2
    core = lax.axis_index("c")
    chip = lax.axis_index(CHIPS)
    other = 1 - core
    first = core == 0

    yh = lax.axis_index("yh")
    turned = (yh - jnp.arange(n_yh, dtype=jnp.int32)) % n_yh

    def around(value):
        return [value] + [
            lax.ppermute(value, "yh", [(i, (i + s) % n_yh) for i in range(n_yh)]) for s in range(1, n_yh)
        ]

    def ordered(own, others):
        return jnp.where(first, own, others), jnp.where(first, others, own)

    upper = jnp.concatenate([up.T, jnp.zeros((rank, block - out_block), BF)], axis=1)
    joined = gather(jnp.concatenate([attention, down.T, upper], axis=0), "z", n_z)
    proj = jnp.concatenate(around(output_projection), axis=1)
    draft_weight_other = swap(draft_weight)
    pad = jnp.broadcast_to(gain[None], (16, block))
    kept = swap(jnp.concatenate([half(residual, other, mine), pad], axis=0))
    residual_parts = ordered(half(residual, core, mine), kept[:mine])
    gain_parts = ordered(gain[None], kept[mine : mine + 1])

    rows = n_z * mine
    send = half(joined[:, :tokens], other, mine, 1).reshape(rows, block)
    keep = half(joined[:, :tokens], core, mine, 1).reshape(rows, block)
    sent = swap(dot("tk,kn->tn", send, proj).astype(BF))
    pair = (dot("tk,kn->tn", keep, proj) + sent.astype(F32)).astype(BF)
    adapters = jnp.concatenate(
        [joined[:, tokens : tokens + rank], joined[:, tokens + rank :, :out_block]], axis=2
    ).reshape(n_z * rank, block + out_block)
    pair, adapters = lax.optimization_barrier((pair, adapters))

    summed = jnp.sum(exchange(pair.reshape(n_chips, mine, n_yh * cols), CHIPS).astype(F32), axis=0).astype(BF)
    summed = jnp.stack([summed[:, s * cols : (s + 1) * cols] for s in range(n_yh)])
    projected = lax.ppermute(
        summed[turned],
        ("z", "yl", "x"),
        [(z * n_chips + k, k * n_chips + z) for z in range(n_z) for k in range(n_chips)],
    )

    adapters_all = jnp.stack(around(adapters))[turned].reshape(tenants * rank, block + out_block)
    adapters_other = swap(adapters_all)
    down_parts = ordered(adapters_all[:, :block], adapters_other[:, :block])
    ups = jnp.concatenate([adapters_all[:, block:], adapters_other[:, block:]], axis=1)

    half_yh = n_yh // 2
    scaled, squares = [], 0.0
    for part in range(2):
        piece = jnp.concatenate(
            [projected[half_yh * part + j] for j in range(half_yh)], axis=1
        ).astype(F32)
        hidden = residual_parts[part].astype(F32) + piece
        squares = squares + jnp.sum(hidden * hidden, axis=1, keepdims=True)
        scaled.append((hidden * gain_parts[part].astype(F32)).astype(BF))
    own_scaled = jnp.where(first, scaled[0], scaled[1])
    partner_scaled = swap(jnp.where(first, scaled[1], scaled[0]))

    slot = jnp.arange(tenants * rank, dtype=jnp.int32) // rank
    slot_tenant = (slot % n_z) * n_yh + slot // n_z
    own_tenant = half(tenant_of, core, mine)
    partner_tenant = half(tenant_of, other, mine)
    own_mask = slot_tenant[:, None] == own_tenant[None, :]
    partner_mask = slot_tenant[:, None] == partner_tenant[None, :]

    def select(values):
        chosen = jnp.where(own_mask, values, 0.0)
        return jnp.sum(chosen.reshape(tenants, rank, mine), axis=0)

    def widen(values, mask):
        return jnp.where(mask, jnp.tile(values, (tenants, 1)), BF(0))

    low_part = select(dot("jd,td->jt", down_parts[0], scaled[0]) + dot("jd,td->jt", down_parts[1], scaled[1]))
    extras = jnp.concatenate(split(low_part), axis=0).T
    message = jnp.concatenate(
        scaled + [extras, *split(squares), jnp.zeros((mine, 128 - 2 * rank - 2), BF)], axis=1
    )
    received = gather(message, CHIPS, n_chips)
    features = received[:, :, : 2 * block]
    totals = jnp.sum(received[:, :, 2 * block :].astype(F32), axis=0)
    square_column = totals[:, 2 * rank : 2 * rank + 1] + totals[:, 2 * rank + 1 : 2 * rank + 2]
    inv_column = lax.rsqrt(square_column / width + EPSILON)
    totals = totals.T
    inv_row = lax.rsqrt((totals[2 * rank : 2 * rank + 1] + totals[2 * rank + 1 : 2 * rank + 2]) / width + EPSILON)
    low_round = ((totals[:rank] + totals[rank : 2 * rank]) * inv_row).astype(BF)
    low_wide = widen(low_round, own_mask)

    target = lax.dynamic_slice(
        features, (chip // 2, 0, (chip % 2) * 2 * out_block), (1, mine, 2 * out_block)
    )[0]
    target = (target.astype(F32) * inv_column).astype(BF)
    next_row = swap(target[:16])[:1]
    target = jnp.concatenate([target[1:], next_row], axis=0)
    target = jnp.concatenate([half(target, core, out_block, 1), half(target, other, out_block, 1)], axis=1)

    following = jnp.roll(tenant_of, -1)
    position = jnp.arange(tokens, dtype=jnp.int32)
    keep_mask = (position < tokens - 1) & (tenant_of == following)
    is_tenant = tenant_of[:, None] == jnp.arange(tenants, dtype=jnp.int32)[None, :]
    count = jnp.sum(jnp.where(is_tenant, tenant_count.astype(F32)[None, :], 0.0), axis=1)
    weight = half(keep_mask.astype(F32) / count, core, mine)[:, None]

    both_weights = jnp.concatenate([draft_weight, draft_weight_other], axis=1)
    draft = dot("ktd,kdn->tn", features, both_weights.reshape(n_chips, 2 * block, 2 * out_block)) * inv_column
    draft = draft + ADAPTER_SCALE * dot("jt,jn->tn", low_wide, ups)
    grad = ((draft - target.astype(F32)) * weight).astype(BF)
    grad_own = grad[:, :out_block]

    back_part = select(dot("jc,tc->jt", ups, grad))
    low_lanes = jnp.concatenate([low_round.T, *split(inv_column), jnp.zeros((mine, 126 - rank), BF)], axis=1)
    partner = jnp.concatenate([grad[:, out_block:], low_lanes], axis=1)
    back_part, partner = lax.optimization_barrier((back_part, partner))
    backs = gather(back_part, MP, 2 * n_chips)
    partner = swap(partner)
    backs = jnp.sum(backs.reshape(n_chips, 2, rank, mine), axis=0)
    partner_codes = partner[:, out_block:].T
    inv_partner = partner_codes[rank : rank + 1].astype(F32) + partner_codes[rank + 1 : rank + 2].astype(F32)
    back_scaled = (ADAPTER_SCALE * half(backs, core, 1)[0] * inv_row).astype(BF)
    back_partner = (ADAPTER_SCALE * half(backs, other, 1)[0] * inv_partner).astype(BF)

    grad_up = dot("jt,tc->jc", low_wide, grad_own) + dot(
        "jt,tc->jc", widen(partner_codes[:rank], partner_mask), partner[:, :out_block]
    )
    grad_down = dot("jt,td->jd", widen(back_scaled, own_mask), own_scaled) + dot(
        "jt,td->jd", widen(back_partner, partner_mask), partner_scaled
    )
    grads = jnp.concatenate([grad_down.astype(BF), grad_up.astype(BF)], axis=1)
    grads = exchange(grads.reshape(tenants, rank, block + out_block), ("yh", "z"))
    grads = jnp.sum(grads.astype(F32), axis=0)
    return grads[:, :block].T, grads[:, block:].T


def solution(mesh):
    split_mesh = Mesh(mesh.devices.reshape(SIZES), AXES)
    return jax.shard_map(
        shards,
        mesh=split_mesh,
        in_specs=(
            P(DP, MP),
            P(MP, DP),
            P(DP, MP),
            P(MP),
            P(None, MP),
            P(MP, DP),
            P(MP, DP),
            P(DP),
            P(),
        ),
        out_specs=(P(MP, DP), P(MP, DP)),
        check_vma=False,
    )
```

```python
import jax
import jax.numpy as jnp
from jax import lax
from jax.sharding import Mesh
from jax.sharding import PartitionSpec as P

EPSILON = 1e-06
ADAPTER_SCALE = 2.0
BF = jnp.bfloat16
F32 = jnp.float32

AXES = ("z", "yh", "yl", "x", "c")
SIZES = (8, 4, 2, 4, 2)
DP = ("z", "yh")
MP = ("yl", "x", "c")
CHIPS = ("yl", "x")


def dot(subscripts, left, right):
    return jnp.einsum(subscripts, left, right, preferred_element_type=F32)


def swap(value):
    return lax.ppermute(value, "c", [(0, 1), (1, 0)])


def exchange(value, axis):
    return lax.all_to_all(value, axis, 0, 0)


def gather(value, axis, size):
    return exchange(jnp.broadcast_to(value[None], (size,) + value.shape), axis)


def split(value):
    high = value.astype(BF)
    return high, (value - high.astype(F32)).astype(BF)


def half(value, which, length, axis=0):
    return lax.dynamic_slice_in_dim(value, which * length, length, axis)


def shards(attention, output_projection, residual, gain, draft_weight, down, up, tenant_of, tenant_count):
    n_z, n_yh, n_yl, n_x, _ = SIZES
    n_chips = n_yl * n_x
    tenants = tenant_count.shape[0]
    rank = down.shape[1]
    tokens, block = residual.shape
    cols = output_projection.shape[1]
    out_block = draft_weight.shape[1]
    width = block * 2 * n_chips
    mine = tokens // 2
    core = lax.axis_index("c")
    chip = lax.axis_index(CHIPS)
    other = 1 - core
    first = core == 0

    yh = lax.axis_index("yh")

    def shift(value, step):
        return lax.ppermute(value, "yh", [(i, (i + step) % n_yh) for i in range(n_yh)])

    def farther(before, after):
        size = before.shape[0] // 2
        return jnp.concatenate([shift(before[:size], 1), shift(after[size:], -1)], axis=0)

    def ordered(own, others):
        return jnp.where(first, own, others), jnp.where(first, others, own)

    upper = jnp.concatenate([up.T, jnp.zeros((rank, block - out_block), BF)], axis=1)
    joined = gather(jnp.concatenate([attention, down.T, upper], axis=0), "z", n_z)
    before, after = shift(output_projection, 1), shift(output_projection, -1)
    proj = jnp.zeros((block, n_yh * cols), BF)
    for step, piece in enumerate([output_projection, before, farther(before, after), after]):
        proj = lax.dynamic_update_slice(proj, piece, (0, (yh - step) % n_yh * cols))
    draft_weight_other = swap(draft_weight)
    pad = jnp.broadcast_to(gain[None], (16, block))
    kept = swap(jnp.concatenate([half(residual, other, mine), pad], axis=0))
    chip_rows = jnp.concatenate(
        ordered(jnp.concatenate([half(residual, core, mine), pad], axis=0), kept), axis=1
    )

    piece = 2 * block // n_chips
    chip_rows = chip_rows.reshape(mine + 16, n_chips, piece).transpose(1, 0, 2)
    joined, chip_rows = lax.optimization_barrier((joined, chip_rows))
    chip_rows = exchange(chip_rows, CHIPS)
    residual_part, gain_part = chip_rows[:, :mine].astype(F32), chip_rows[:, mine : mine + 1].astype(F32)

    rows = n_z * mine
    send = half(joined[:, :tokens], other, mine, 1).reshape(rows, block)
    keep = half(joined[:, :tokens], core, mine, 1).reshape(rows, block)
    sent = swap(dot("tk,kn->tn", send, proj).astype(BF))
    pair = (dot("tk,kn->tn", keep, proj) + sent.astype(F32)).astype(BF)
    pair = pair.reshape(rows, n_chips, piece).transpose(1, 0, 2)
    summed = jnp.sum(exchange(pair, CHIPS).astype(F32), axis=0).astype(BF)
    adapters = jnp.concatenate(
        [joined[:, tokens : tokens + rank], joined[:, tokens + rank :, :out_block]], axis=2
    ).reshape(n_z * rank, block + out_block)
    summed, adapters = lax.optimization_barrier((summed, adapters))
    projected = exchange(summed.reshape(n_z, mine, piece), "z").astype(F32)
    before, after = shift(adapters, 1), shift(adapters, -1)

    hidden = residual_part + projected
    squares = jnp.sum(jnp.sum(hidden * hidden, axis=0), axis=1, keepdims=True)
    scaled = (hidden * gain_part).astype(BF)
    message = jnp.concatenate(
        [scaled[z] for z in range(n_z)] + [*split(squares), jnp.zeros((mine, 126), BF)], axis=1
    )
    message, before, after = lax.optimization_barrier((message, before, after))
    received = gather(message, CHIPS, n_chips)
    features = received[:, :, : 2 * block].reshape(n_chips, mine, n_z, piece)
    features = features.transpose(2, 1, 0, 3).reshape(n_z, mine, 2 * block)
    totals = jnp.sum(received[:, :, 2 * block :].astype(F32), axis=0)
    inv_column = lax.rsqrt((totals[:, :1] + totals[:, 1:2]) / width + EPSILON)
    inv_row = jnp.broadcast_to(inv_column, (mine, 128)).T[:1]

    adapters_all = jnp.zeros((n_yh, n_z * rank, block + out_block), BF)
    for step, part in enumerate([adapters, before, farther(before, after), after]):
        adapters_all = lax.dynamic_update_slice(adapters_all, part[None], ((yh - step) % n_yh, 0, 0))
    adapters_all = adapters_all.reshape(tenants * rank, block + out_block)
    adapters_other = swap(adapters_all)
    downs = jnp.concatenate(ordered(adapters_all[:, :block], adapters_other[:, :block]), axis=1)
    ups = jnp.concatenate([adapters_all[:, block:], adapters_other[:, block:]], axis=1)

    slot = jnp.arange(tenants * rank, dtype=jnp.int32) // rank
    slot_tenant = (slot % n_z) * n_yh + slot // n_z
    own_tenant = half(tenant_of, core, mine)
    partner_tenant = half(tenant_of, other, mine)
    own_mask = slot_tenant[:, None] == own_tenant[None, :]
    partner_mask = slot_tenant[:, None] == partner_tenant[None, :]

    def select(values):
        chosen = jnp.where(own_mask, values, 0.0)
        return jnp.sum(chosen.reshape(tenants, rank, mine), axis=0)

    def widen(values, mask):
        return jnp.where(mask, jnp.tile(values, (tenants, 1)), BF(0))

    chip_features = lax.dynamic_index_in_dim(features, chip, 0, keepdims=False)
    own_scaled = half(chip_features, core, block, 1)
    low_part = select(dot("jd,td->jt", downs, chip_features))
    low_round = (jnp.sum(gather(low_part, CHIPS, n_chips), axis=0) * inv_row).astype(BF)
    partner_scaled = swap(half(chip_features, other, block, 1))
    low_wide = widen(low_round, own_mask)

    target = lax.dynamic_slice(
        features, (chip // 2, 0, (chip % 2) * 2 * out_block), (1, mine, 2 * out_block)
    )[0]
    target = (target.astype(F32) * inv_column).astype(BF)
    next_row = swap(target[:16])[:1]
    target = jnp.concatenate([target[1:], next_row], axis=0)
    target = jnp.concatenate([half(target, core, out_block, 1), half(target, other, out_block, 1)], axis=1)

    following = jnp.roll(tenant_of, -1)
    position = jnp.arange(tokens, dtype=jnp.int32)
    keep_mask = (position < tokens - 1) & (tenant_of == following)
    is_tenant = tenant_of[:, None] == jnp.arange(tenants, dtype=jnp.int32)[None, :]
    count = jnp.sum(jnp.where(is_tenant, tenant_count.astype(F32)[None, :], 0.0), axis=1)
    weight = half(keep_mask.astype(F32) / count, core, mine)[:, None]

    both_weights = jnp.concatenate([draft_weight, draft_weight_other], axis=1)
    draft = dot("ktd,kdn->tn", features, both_weights.reshape(n_chips, 2 * block, 2 * out_block)) * inv_column
    draft = draft + ADAPTER_SCALE * dot("jt,jn->tn", low_wide, ups)
    grad = ((draft - target.astype(F32)) * weight).astype(BF)
    grad_own = grad[:, :out_block]

    back_part = select(dot("jc,tc->jt", ups, grad))
    low_lanes = jnp.concatenate([low_round.T, *split(inv_column), jnp.zeros((mine, 126 - rank), BF)], axis=1)
    partner = jnp.concatenate([grad[:, out_block:], low_lanes], axis=1)
    back_part, partner = lax.optimization_barrier((back_part, partner))
    backs = gather(back_part, MP, 2 * n_chips)
    partner = swap(partner)
    backs = jnp.sum(backs.reshape(n_chips, 2, rank, mine), axis=0)
    partner_codes = partner[:, out_block:].T
    inv_partner = partner_codes[rank : rank + 1].astype(F32) + partner_codes[rank + 1 : rank + 2].astype(F32)
    back_scaled = (ADAPTER_SCALE * half(backs, core, 1)[0] * inv_row).astype(BF)
    back_partner = (ADAPTER_SCALE * half(backs, other, 1)[0] * inv_partner).astype(BF)

    grad_up = dot("jt,tc->jc", low_wide, grad_own) + dot(
        "jt,tc->jc", widen(partner_codes[:rank], partner_mask), partner[:, :out_block]
    )
    grad_down = dot("jt,td->jd", widen(back_scaled, own_mask), own_scaled) + dot(
        "jt,td->jd", widen(back_partner, partner_mask), partner_scaled
    )
    grads = jnp.concatenate([grad_down.astype(BF), grad_up.astype(BF)], axis=1)
    grads = exchange(grads.reshape(tenants, rank, block + out_block), ("yh", "z"))
    grads = jnp.sum(grads.astype(F32), axis=0)
    return grads[:, :block].T, grads[:, block:].T


def solution(mesh):
    split_mesh = Mesh(mesh.devices.reshape(SIZES), AXES)
    return jax.shard_map(
        shards,
        mesh=split_mesh,
        in_specs=(
            P(DP, MP),
            P(MP, DP),
            P(DP, MP),
            P(MP),
            P(None, MP),
            P(MP, DP),
            P(MP, DP),
            P(DP),
            P(),
        ),
        out_specs=(P(MP, DP), P(MP, DP)),
        check_vma=False,
    )
```

```python
import jax
import jax.numpy as jnp
from jax import lax
from jax.sharding import Mesh
from jax.sharding import PartitionSpec as P

EPSILON = 1e-06
ADAPTER_SCALE = 2.0
BF = jnp.bfloat16
F32 = jnp.float32

AXES = ("z", "yh", "yl", "x", "c")
SIZES = (8, 4, 2, 4, 2)
DP = ("z", "yh")
MP = ("yl", "x", "c")
CHIPS = ("yl", "x")


def dot(subscripts, left, right):
    return jnp.einsum(subscripts, left, right, preferred_element_type=F32)


def swap(value):
    return lax.ppermute(value, "c", [(0, 1), (1, 0)])


def exchange(value, axis):
    return lax.all_to_all(value, axis, 0, 0)


def gather(value, axis, size):
    return exchange(jnp.broadcast_to(value[None], (size,) + value.shape), axis)


def split(value):
    high = value.astype(BF)
    return high, (value - high.astype(F32)).astype(BF)


def half(value, which, length, axis=0):
    return lax.dynamic_slice_in_dim(value, which * length, length, axis)


def shards(attention, output_projection, residual, gain, draft_weight, down, up, tenant_of, tenant_count):
    n_z, n_yh, n_yl, n_x, _ = SIZES
    n_chips = n_yl * n_x
    tenants = tenant_count.shape[0]
    rank = down.shape[1]
    tokens, block = residual.shape
    cols = output_projection.shape[1]
    out_block = draft_weight.shape[1]
    width = block * 2 * n_chips
    mine = tokens // 2
    core = lax.axis_index("c")
    chip = lax.axis_index(CHIPS)
    other = 1 - core
    first = core == 0

    yh = lax.axis_index("yh")

    def shift(value, step):
        return lax.ppermute(value, "yh", [(i, (i + step) % n_yh) for i in range(n_yh)])

    def ordered(own, others):
        return jnp.where(first, own, others), jnp.where(first, others, own)

    upper = jnp.concatenate([up.T, jnp.zeros((rank, block - out_block), BF)], axis=1)
    joined = gather(jnp.concatenate([attention, down.T, upper], axis=0), "z", n_z)
    proj = jnp.zeros((block, n_yh * cols), BF)
    for step in range(n_yh):
        part = shift(output_projection, step) if step else output_projection
        proj = lax.dynamic_update_slice(proj, part, (0, (yh - step) % n_yh * cols))
    both_weights = jnp.concatenate([draft_weight, swap(draft_weight)], axis=1)
    pad = jnp.broadcast_to(gain[None], (16, block))
    kept = swap(jnp.concatenate([half(residual, other, mine), pad], axis=0))
    chip_rows = jnp.concatenate(
        ordered(jnp.concatenate([half(residual, core, mine), pad], axis=0), kept), axis=1
    )

    piece = 2 * block // n_chips
    chip_rows = chip_rows.reshape(mine + 16, n_chips, piece).transpose(1, 0, 2)
    joined, chip_rows, both_weights = lax.optimization_barrier((joined, chip_rows, both_weights))
    chip_rows = exchange(chip_rows, CHIPS)
    residual_part, gain_part = chip_rows[:, :mine].astype(F32), chip_rows[:, mine : mine + 1].astype(F32)

    rows = n_z * mine
    send = half(joined[:, :tokens], other, mine, 1).reshape(rows, block)
    keep = half(joined[:, :tokens], core, mine, 1).reshape(rows, block)
    sent = swap(dot("tk,kn->tn", send, proj).astype(BF))
    pair = (dot("tk,kn->tn", keep, proj) + sent.astype(F32)).astype(BF)
    pair = pair.reshape(rows, n_chips, piece).transpose(1, 0, 2)
    adapters = jnp.concatenate(
        [joined[:, tokens : tokens + rank], joined[:, tokens + rank :, :out_block]], axis=2
    ).reshape(n_z * rank, block + out_block)
    pair, adapters, residual_part, gain_part = lax.optimization_barrier((pair, adapters, residual_part, gain_part))
    summed = jnp.sum(exchange(pair, CHIPS).astype(F32), axis=0).astype(BF)
    adapters_parts = [adapters] + [shift(adapters, step) for step in range(1, n_yh)]
    projected = exchange(summed.reshape(n_z, mine, piece), "z").astype(F32)

    hidden = residual_part + projected
    squares = jnp.sum(jnp.sum(hidden * hidden, axis=0), axis=1, keepdims=True)
    scaled = (hidden * gain_part).astype(BF)
    message = jnp.concatenate(
        [scaled[z] for z in range(n_z)] + [*split(squares), jnp.zeros((mine, 126), BF)], axis=1
    )
    message, *adapters_parts = lax.optimization_barrier((message, *adapters_parts))
    received = gather(message, CHIPS, n_chips)
    features = received[:, :, : 2 * block].reshape(n_chips, mine, n_z, piece)
    features = features.transpose(2, 1, 0, 3).reshape(n_z, mine, 2 * block)
    totals = jnp.sum(received[:, :, 2 * block :].astype(F32), axis=0)
    inv_column = lax.rsqrt((totals[:, :1] + totals[:, 1:2]) / width + EPSILON)
    inv_row = jnp.broadcast_to(inv_column, (mine, 128)).T[:1]

    adapters_all = jnp.zeros((n_yh, n_z * rank, block + out_block), BF)
    for step, part in enumerate(adapters_parts):
        adapters_all = lax.dynamic_update_slice(adapters_all, part[None], ((yh - step) % n_yh, 0, 0))
    adapters_all = adapters_all.reshape(tenants * rank, block + out_block)
    adapters_other = swap(adapters_all)
    downs = jnp.concatenate(ordered(adapters_all[:, :block], adapters_other[:, :block]), axis=1)
    ups = jnp.concatenate([adapters_all[:, block:], adapters_other[:, block:]], axis=1)

    slot = jnp.arange(tenants * rank, dtype=jnp.int32) // rank
    slot_tenant = (slot % n_z) * n_yh + slot // n_z
    own_tenant = half(tenant_of, core, mine)
    partner_tenant = half(tenant_of, other, mine)
    own_mask = slot_tenant[:, None] == own_tenant[None, :]
    partner_mask = slot_tenant[:, None] == partner_tenant[None, :]

    def select(values):
        chosen = jnp.where(own_mask, values, 0.0)
        return jnp.sum(chosen.reshape(tenants, rank, mine), axis=0)

    def widen(values, mask):
        return jnp.where(mask, jnp.tile(values, (tenants, 1)), BF(0))

    chip_features = lax.dynamic_index_in_dim(features, chip, 0, keepdims=False)
    own_scaled = half(chip_features, core, block, 1)
    low_part = select(dot("jd,td->jt", downs, chip_features))
    low_round = (jnp.sum(gather(low_part, CHIPS, n_chips), axis=0) * inv_row).astype(BF)
    partner_scaled = swap(half(chip_features, other, block, 1))
    low_wide = widen(low_round, own_mask)

    target = lax.dynamic_slice(
        features, (chip // 2, 0, (chip % 2) * 2 * out_block), (1, mine, 2 * out_block)
    )[0]
    target = (target.astype(F32) * inv_column).astype(BF)
    next_row = swap(target[:16])[:1]
    target = jnp.concatenate([target[1:], next_row], axis=0)
    target = jnp.concatenate([half(target, core, out_block, 1), half(target, other, out_block, 1)], axis=1)

    following = jnp.roll(tenant_of, -1)
    position = jnp.arange(tokens, dtype=jnp.int32)
    keep_mask = (position < tokens - 1) & (tenant_of == following)
    is_tenant = tenant_of[:, None] == jnp.arange(tenants, dtype=jnp.int32)[None, :]
    count = jnp.sum(jnp.where(is_tenant, tenant_count.astype(F32)[None, :], 0.0), axis=1)
    weight = half(keep_mask.astype(F32) / count, core, mine)[:, None]

    draft = dot("ktd,kdn->tn", features, both_weights.reshape(n_chips, 2 * block, 2 * out_block))
    draft, low_wide = lax.optimization_barrier((draft, low_wide))
    draft = draft * inv_column + ADAPTER_SCALE * dot("jt,jn->tn", low_wide, ups)
    grad = ((draft - target.astype(F32)) * weight).astype(BF)
    grad_own = grad[:, :out_block]

    back_part = select(dot("jc,tc->jt", ups, grad))
    low_lanes = jnp.concatenate([low_round.T, *split(inv_column), jnp.zeros((mine, 126 - rank), BF)], axis=1)
    partner = jnp.concatenate([grad[:, out_block:], low_lanes], axis=1)
    back_part, partner = lax.optimization_barrier((back_part, partner))
    backs = gather(back_part, MP, 2 * n_chips)
    partner = swap(partner)
    backs = jnp.sum(backs.reshape(n_chips, 2, rank, mine), axis=0)
    partner_codes = partner[:, out_block:].T
    inv_partner = partner_codes[rank : rank + 1].astype(F32) + partner_codes[rank + 1 : rank + 2].astype(F32)
    back_scaled = (ADAPTER_SCALE * half(backs, core, 1)[0] * inv_row).astype(BF)
    back_partner = (ADAPTER_SCALE * half(backs, other, 1)[0] * inv_partner).astype(BF)

    grad_up = dot("jt,tc->jc", low_wide, grad_own) + dot(
        "jt,tc->jc", widen(partner_codes[:rank], partner_mask), partner[:, :out_block]
    )
    grad_down = dot("jt,td->jd", widen(back_scaled, own_mask), own_scaled) + dot(
        "jt,td->jd", widen(back_partner, partner_mask), partner_scaled
    )
    grads = jnp.concatenate([grad_down.astype(BF), grad_up.astype(BF)], axis=1)
    grads = exchange(grads.reshape(tenants, rank, block + out_block), ("yh", "z"))
    grads = jnp.sum(grads.astype(F32), axis=0)
    return grads[:, :block].T, grads[:, block:].T


def solution(mesh):
    split_mesh = Mesh(mesh.devices.reshape(SIZES), AXES)
    return jax.shard_map(
        shards,
        mesh=split_mesh,
        in_specs=(
            P(DP, MP),
            P(MP, DP),
            P(DP, MP),
            P(MP),
            P(None, MP),
            P(MP, DP),
            P(MP, DP),
            P(DP),
            P(),
        ),
        out_specs=(P(MP, DP), P(MP, DP)),
        check_vma=False,
    )
```

```python
import jax
import jax.numpy as jnp
from jax import lax
from jax.sharding import Mesh
from jax.sharding import PartitionSpec as P

EPSILON = 1e-06
ADAPTER_SCALE = 2.0
BF = jnp.bfloat16
F32 = jnp.float32

AXES = ("z", "yh", "yl", "x", "c")
SIZES = (8, 4, 2, 4, 2)
DP = ("z", "yh")
MP = ("yl", "x", "c")
CHIPS = ("yl", "x")


def dot(subscripts, left, right):
    return jnp.einsum(subscripts, left, right, preferred_element_type=F32)


def swap(value):
    return lax.ppermute(value, "c", [(0, 1), (1, 0)])


def exchange(value, axis):
    return lax.all_to_all(value, axis, 0, 0)


def gather(value, axis, size):
    return exchange(jnp.broadcast_to(value[None], (size,) + value.shape), axis)


def split(value):
    high = value.astype(BF)
    return high, (value - high.astype(F32)).astype(BF)


def half(value, which, length, axis=0):
    return lax.dynamic_slice_in_dim(value, which * length, length, axis)


def shards(attention, output_projection, residual, gain, draft_weight, down, up, tenant_of, tenant_count):
    n_z, n_yh, n_yl, n_x, _ = SIZES
    n_chips = n_yl * n_x
    tenants = tenant_count.shape[0]
    rank = down.shape[1]
    tokens, block = residual.shape
    cols = output_projection.shape[1]
    out_block = draft_weight.shape[1]
    width = block * 2 * n_chips
    mine = tokens // 2
    core = lax.axis_index("c")
    chip = lax.axis_index(CHIPS)
    other = 1 - core
    first = core == 0

    def ordered(own, others):
        return jnp.where(first, own, others), jnp.where(first, others, own)

    upper = jnp.concatenate([up.T, jnp.zeros((rank, block - out_block), BF)], axis=1)
    joined = lax.all_gather(jnp.concatenate([attention, down.T, upper], axis=0), "z", axis=0)
    pieces = gather(output_projection, "yh", n_yh)
    proj = jnp.concatenate([pieces[j] for j in range(n_yh)], axis=1)
    draft_weight_other = swap(draft_weight)
    pad = jnp.broadcast_to(gain[None], (16, block))
    kept = swap(jnp.concatenate([half(residual, other, mine), pad], axis=0))
    residual_parts = ordered(half(residual, core, mine), kept[:mine])
    gain_parts = ordered(gain[None], kept[mine : mine + 1])

    adapters = jnp.concatenate(
        [joined[:, tokens : tokens + rank], joined[:, tokens + rank :]], axis=2
    ).reshape(n_z * rank, 2 * block)
    adapters_all = lax.all_gather(adapters, "yh", axis=0).reshape(tenants * rank, 2 * block)
    adapters_all = adapters_all[:, : block + out_block]
    adapters_other = swap(adapters_all)
    down_parts = ordered(adapters_all[:, :block], adapters_other[:, :block])
    ups = jnp.concatenate([adapters_all[:, block:], adapters_other[:, block:]], axis=1)

    z = lax.axis_index("z")
    order = (z + jnp.arange(n_z, dtype=jnp.int32)) % n_z
    rows = n_z * mine
    send = half(joined[:, :tokens], other, mine, 1)[order].reshape(rows, block)
    keep = half(joined[:, :tokens], core, mine, 1)[order].reshape(rows, block)
    sent = swap(dot("tk,kn->tn", send, proj).astype(BF))
    pair = (dot("tk,kn->tn", keep, proj) + sent.astype(F32)).astype(BF)

    summed = jnp.sum(exchange(pair.reshape(n_chips, mine, n_yh * cols), CHIPS).astype(F32), axis=0).astype(BF)
    places = [(i, k) for i in range(n_z) for k in range(n_chips)]
    homes = [(i * n_chips + k, (i + k) % n_z * n_chips + k) for i, k in places]
    chips = [(i * n_chips + k, i * n_chips + (i - k) % n_chips) for i, k in places]
    projected = lax.ppermute(lax.ppermute(summed, ("z", "yl", "x"), homes), ("z", "yl", "x"), chips)

    scaled, squares = [], 0.0
    for part in range(2):
        piece = projected[:, part * block : (part + 1) * block].astype(F32)
        hidden = residual_parts[part].astype(F32) + piece
        squares = squares + jnp.sum(hidden * hidden, axis=1, keepdims=True)
        scaled.append((hidden * gain_parts[part].astype(F32)).astype(BF))
    own_scaled = jnp.where(first, scaled[0], scaled[1])
    partner_scaled = swap(jnp.where(first, scaled[1], scaled[0]))

    slot = jnp.arange(tenants * rank, dtype=jnp.int32) // rank
    slot_tenant = (slot % n_z) * n_yh + slot // n_z
    own_tenant = half(tenant_of, core, mine)
    partner_tenant = half(tenant_of, other, mine)
    own_mask = slot_tenant[:, None] == own_tenant[None, :]
    partner_mask = slot_tenant[:, None] == partner_tenant[None, :]

    def select(values):
        chosen = jnp.where(own_mask, values, 0.0)
        return jnp.sum(chosen.reshape(tenants, rank, mine), axis=0)

    def widen(values, mask):
        return jnp.where(mask, jnp.tile(values, (tenants, 1)), BF(0))

    low_part = select(dot("jd,td->jt", down_parts[0], scaled[0]) + dot("jd,td->jt", down_parts[1], scaled[1]))
    extras = jnp.concatenate(split(low_part), axis=0).T
    message = jnp.concatenate(
        scaled + [extras, *split(squares), jnp.zeros((mine, 128 - 2 * rank - 2), BF)], axis=1
    )
    received = gather(message, CHIPS, n_chips)
    features = received[:, :, : 2 * block]
    totals = jnp.sum(received[:, :, 2 * block :].astype(F32), axis=0)
    square_column = totals[:, 2 * rank : 2 * rank + 1] + totals[:, 2 * rank + 1 : 2 * rank + 2]
    inv_column = lax.rsqrt(square_column / width + EPSILON)
    totals = totals.T
    inv_row = lax.rsqrt((totals[2 * rank : 2 * rank + 1] + totals[2 * rank + 1 : 2 * rank + 2]) / width + EPSILON)
    low_round = ((totals[:rank] + totals[rank : 2 * rank]) * inv_row).astype(BF)
    low_wide = widen(low_round, own_mask)

    target = lax.dynamic_slice(
        features, (chip // 2, 0, (chip % 2) * 2 * out_block), (1, mine, 2 * out_block)
    )[0]
    target = (target.astype(F32) * inv_column).astype(BF)
    next_row = swap(target[:16])[:1]
    target = jnp.concatenate([target[1:], next_row], axis=0)
    target = jnp.concatenate([half(target, core, out_block, 1), half(target, other, out_block, 1)], axis=1)

    following = jnp.roll(tenant_of, -1)
    position = jnp.arange(tokens, dtype=jnp.int32)
    keep_mask = (position < tokens - 1) & (tenant_of == following)
    is_tenant = tenant_of[:, None] == jnp.arange(tenants, dtype=jnp.int32)[None, :]
    count = jnp.sum(jnp.where(is_tenant, tenant_count.astype(F32)[None, :], 0.0), axis=1)
    weight = half(keep_mask.astype(F32) / count, core, mine)[:, None]

    both_weights = jnp.concatenate([draft_weight, draft_weight_other], axis=1)
    draft = dot("ktd,kdn->tn", features, both_weights.reshape(n_chips, 2 * block, 2 * out_block)) * inv_column
    draft = draft + ADAPTER_SCALE * dot("jt,jn->tn", low_wide, ups)
    grad = ((draft - target.astype(F32)) * weight).astype(BF)
    grad_own = grad[:, :out_block]

    back_part = select(dot("jc,tc->jt", ups, grad))
    low_lanes = jnp.concatenate([low_round.T, *split(inv_column), jnp.zeros((mine, 126 - rank), BF)], axis=1)
    partner = jnp.concatenate([grad[:, out_block:], low_lanes], axis=1)
    back_part, partner = lax.optimization_barrier((back_part, partner))
    backs = gather(back_part, MP, 2 * n_chips)
    partner = swap(partner)
    backs = jnp.sum(backs.reshape(n_chips, 2, rank, mine), axis=0)
    partner_codes = partner[:, out_block:].T
    inv_partner = partner_codes[rank : rank + 1].astype(F32) + partner_codes[rank + 1 : rank + 2].astype(F32)
    back_scaled = (ADAPTER_SCALE * half(backs, core, 1)[0] * inv_row).astype(BF)
    back_partner = (ADAPTER_SCALE * half(backs, other, 1)[0] * inv_partner).astype(BF)

    grad_up = dot("jt,tc->jc", low_wide, grad_own) + dot(
        "jt,tc->jc", widen(partner_codes[:rank], partner_mask), partner[:, :out_block]
    )
    grad_down = dot("jt,td->jd", widen(back_scaled, own_mask), own_scaled) + dot(
        "jt,td->jd", widen(back_partner, partner_mask), partner_scaled
    )
    grads = jnp.concatenate([grad_down.astype(BF), grad_up.astype(BF)], axis=1)
    grads = exchange(grads.reshape(tenants, rank, block + out_block), ("yh", "z"))
    grads = jnp.sum(grads.astype(F32), axis=0)
    return grads[:, :block].T, grads[:, block:].T


def solution(mesh):
    split_mesh = Mesh(mesh.devices.reshape(SIZES), AXES)
    return jax.shard_map(
        shards,
        mesh=split_mesh,
        in_specs=(
            P(DP, MP),
            P(MP, DP),
            P(DP, MP),
            P(MP),
            P(None, MP),
            P(MP, DP),
            P(MP, DP),
            P(DP),
            P(),
        ),
        out_specs=(P(MP, DP), P(MP, DP)),
        check_vma=False,
    )
```

```python
import jax
import jax.numpy as jnp
from jax import lax
from jax.sharding import Mesh
from jax.sharding import PartitionSpec as P

EPSILON = 1e-06
ADAPTER_SCALE = 2.0
BF = jnp.bfloat16
F32 = jnp.float32

AXES = ("z", "yh", "yl", "x", "c")
SIZES = (8, 4, 2, 4, 2)
DP = ("z", "yh")
MP = ("yl", "x", "c")
CHIPS = ("yl", "x")


def dot(subscripts, left, right):
    return jnp.einsum(subscripts, left, right, preferred_element_type=F32)


def swap(value):
    return lax.ppermute(value, "c", [(0, 1), (1, 0)])


def exchange(value, axis):
    return lax.all_to_all(value, axis, 0, 0)


def gather(value, axis, size):
    return exchange(jnp.broadcast_to(value[None], (size,) + value.shape), axis)


def split(value):
    high = value.astype(BF)
    return high, (value - high.astype(F32)).astype(BF)


def half(value, which, length, axis=0):
    return lax.dynamic_slice_in_dim(value, which * length, length, axis)


def shards(attention, output_projection, residual, gain, draft_weight, down, up, tenant_of, tenant_count):
    n_z, n_yh, n_yl, n_x, _ = SIZES
    n_chips = n_yl * n_x
    tenants = tenant_count.shape[0]
    rank = down.shape[1]
    tokens, block = residual.shape
    cols = output_projection.shape[1]
    out_block = draft_weight.shape[1]
    width = block * 2 * n_chips
    mine = tokens // 2
    core = lax.axis_index("c")
    chip = lax.axis_index(CHIPS)
    other = 1 - core
    first = core == 0

    yh = lax.axis_index("yh")
    turned = (yh - jnp.arange(n_yh, dtype=jnp.int32)) % n_yh

    def around(value):
        return [value] + [
            lax.ppermute(value, "yh", [(i, (i + s) % n_yh) for i in range(n_yh)]) for s in range(1, n_yh)
        ]

    def ordered(own, others):
        return jnp.where(first, own, others), jnp.where(first, others, own)

    upper = jnp.concatenate([up.T, jnp.zeros((rank, block - out_block), BF)], axis=1)
    joined = gather(jnp.concatenate([attention, down.T, upper], axis=0), "z", n_z)
    proj = jnp.concatenate(around(output_projection), axis=1)
    draft_weight_other = swap(draft_weight)
    pad = jnp.broadcast_to(gain[None], (16, block))
    kept = swap(jnp.concatenate([half(residual, other, mine), pad], axis=0))
    chip_rows = jnp.concatenate(
        ordered(jnp.concatenate([half(residual, core, mine), pad], axis=0), kept), axis=1
    )
    places = [(i, k) for i in range(n_z) for k in range(n_chips)]
    homes = [(i * n_chips + k, (i + k) % n_z * n_chips + k) for i, k in places]
    chips = [(i * n_chips + k, i * n_chips + (i - k) % n_chips) for i, k in places]
    chip_rows = lax.ppermute(chip_rows, ("z", "yl", "x"), chips)
    joined, chip_rows = lax.optimization_barrier((joined, chip_rows))
    residual_part, gain_part = chip_rows[:mine].astype(F32), chip_rows[mine : mine + 1].astype(F32)

    rows = n_z * mine
    z = lax.axis_index("z")
    order = (z + jnp.arange(n_z, dtype=jnp.int32)) % n_z
    send = half(joined[:, :tokens], other, mine, 1)[order].reshape(rows, block)
    keep = half(joined[:, :tokens], core, mine, 1)[order].reshape(rows, block)
    sent = swap(dot("tk,kn->tn", send, proj).astype(BF))
    pair = (dot("tk,kn->tn", keep, proj) + sent.astype(F32)).astype(BF)
    adapters = jnp.concatenate(
        [joined[:, tokens : tokens + rank], joined[:, tokens + rank :, :out_block]], axis=2
    ).reshape(n_z * rank, block + out_block)
    pair, adapters = lax.optimization_barrier((pair, adapters))
    parts = around(adapters)

    summed = jnp.sum(exchange(pair.reshape(n_chips, mine, n_yh * cols), CHIPS).astype(F32), axis=0).astype(BF)
    summed, parts[1], parts[3] = lax.optimization_barrier((summed, parts[1], parts[3]))
    summed = jnp.stack([summed[:, s * cols : (s + 1) * cols] for s in range(n_yh)])
    projected = lax.ppermute(summed[turned], ("z", "yl", "x"), homes)
    projected, parts[2] = lax.optimization_barrier((projected, parts[2]))

    hidden = residual_part + jnp.concatenate([projected[j] for j in range(n_yh)], axis=1).astype(F32)
    squares = jnp.sum(hidden * hidden, axis=1, keepdims=True)
    scaled = (hidden * gain_part).astype(BF)
    message = jnp.concatenate([scaled, *split(squares), jnp.zeros((mine, 126), BF)], axis=1)
    received = gather(message, CHIPS, n_chips)
    blocks = (z - jnp.arange(n_chips, dtype=jnp.int32)) % n_chips
    features = received[:, :, : 2 * block][blocks]
    totals = jnp.sum(received[:, :, 2 * block :].astype(F32), axis=0)
    inv_column = lax.rsqrt((totals[:, :1] + totals[:, 1:2]) / width + EPSILON)
    inv_row = jnp.broadcast_to(inv_column, (mine, 128)).T[:1]

    adapters_all = jnp.stack(parts)[turned].reshape(tenants * rank, block + out_block)
    adapters_other = swap(adapters_all)
    downs = jnp.concatenate(ordered(adapters_all[:, :block], adapters_other[:, :block]), axis=1)
    ups = jnp.concatenate([adapters_all[:, block:], adapters_other[:, block:]], axis=1)

    slot = jnp.arange(tenants * rank, dtype=jnp.int32) // rank
    slot_tenant = (slot % n_z) * n_yh + slot // n_z
    own_tenant = half(tenant_of, core, mine)
    partner_tenant = half(tenant_of, other, mine)
    own_mask = slot_tenant[:, None] == own_tenant[None, :]
    partner_mask = slot_tenant[:, None] == partner_tenant[None, :]

    def select(values):
        chosen = jnp.where(own_mask, values, 0.0)
        return jnp.sum(chosen.reshape(tenants, rank, mine), axis=0)

    def widen(values, mask):
        return jnp.where(mask, jnp.tile(values, (tenants, 1)), BF(0))

    chip_features = lax.dynamic_index_in_dim(features, chip, 0, keepdims=False)
    own_scaled = half(chip_features, core, block, 1)
    low_part = select(dot("jd,td->jt", downs, chip_features))
    low_round = (jnp.sum(gather(low_part, CHIPS, n_chips), axis=0) * inv_row).astype(BF)
    partner_scaled = swap(half(chip_features, other, block, 1))
    low_wide = widen(low_round, own_mask)

    target = lax.dynamic_slice(
        features, (chip // 2, 0, (chip % 2) * 2 * out_block), (1, mine, 2 * out_block)
    )[0]
    target = (target.astype(F32) * inv_column).astype(BF)
    next_row = swap(target[:16])[:1]
    target = jnp.concatenate([target[1:], next_row], axis=0)
    target = jnp.concatenate([half(target, core, out_block, 1), half(target, other, out_block, 1)], axis=1)

    following = jnp.roll(tenant_of, -1)
    position = jnp.arange(tokens, dtype=jnp.int32)
    keep_mask = (position < tokens - 1) & (tenant_of == following)
    is_tenant = tenant_of[:, None] == jnp.arange(tenants, dtype=jnp.int32)[None, :]
    count = jnp.sum(jnp.where(is_tenant, tenant_count.astype(F32)[None, :], 0.0), axis=1)
    weight = half(keep_mask.astype(F32) / count, core, mine)[:, None]

    both_weights = jnp.concatenate([draft_weight, draft_weight_other], axis=1)
    draft = dot("ktd,kdn->tn", features, both_weights.reshape(n_chips, 2 * block, 2 * out_block))
    draft, low_wide = lax.optimization_barrier((draft, low_wide))
    draft = draft * inv_column + ADAPTER_SCALE * dot("jt,jn->tn", low_wide, ups)
    grad = ((draft - target.astype(F32)) * weight).astype(BF)
    grad_own = grad[:, :out_block]

    back_part = select(dot("jc,tc->jt", ups, grad))
    low_lanes = jnp.concatenate([low_round.T, *split(inv_column), jnp.zeros((mine, 126 - rank), BF)], axis=1)
    partner = jnp.concatenate([grad[:, out_block:], low_lanes], axis=1)
    back_part, partner = lax.optimization_barrier((back_part, partner))
    backs = gather(back_part, MP, 2 * n_chips)
    partner = swap(partner)
    backs = jnp.sum(backs.reshape(n_chips, 2, rank, mine), axis=0)
    partner_codes = partner[:, out_block:].T
    inv_partner = partner_codes[rank : rank + 1].astype(F32) + partner_codes[rank + 1 : rank + 2].astype(F32)
    back_scaled = (ADAPTER_SCALE * half(backs, core, 1)[0] * inv_row).astype(BF)
    back_partner = (ADAPTER_SCALE * half(backs, other, 1)[0] * inv_partner).astype(BF)

    grad_up = dot("jt,tc->jc", low_wide, grad_own) + dot(
        "jt,tc->jc", widen(partner_codes[:rank], partner_mask), partner[:, :out_block]
    )
    grad_down = dot("jt,td->jd", widen(back_scaled, own_mask), own_scaled) + dot(
        "jt,td->jd", widen(back_partner, partner_mask), partner_scaled
    )
    grads = jnp.concatenate([grad_down.astype(BF), grad_up.astype(BF)], axis=1)
    grads = exchange(grads.reshape(tenants, rank, block + out_block), ("yh", "z"))
    grads = jnp.sum(grads.astype(F32), axis=0)
    return grads[:, :block].T, grads[:, block:].T


def solution(mesh):
    split_mesh = Mesh(mesh.devices.reshape(SIZES), AXES)
    return jax.shard_map(
        shards,
        mesh=split_mesh,
        in_specs=(
            P(DP, MP),
            P(MP, DP),
            P(DP, MP),
            P(MP),
            P(None, MP),
            P(MP, DP),
            P(MP, DP),
            P(DP),
            P(),
        ),
        out_specs=(P(MP, DP), P(MP, DP)),
        check_vma=False,
    )
```

```python
import jax
import jax.numpy as jnp
from jax import lax
from jax.sharding import Mesh
from jax.sharding import PartitionSpec as P

EPSILON = 1e-06
ADAPTER_SCALE = 2.0
BF = jnp.bfloat16
F32 = jnp.float32

AXES = ("z", "yh", "yl", "x", "c")
SIZES = (8, 4, 2, 4, 2)
DP = ("z", "yh")
MP = ("yl", "x", "c")
CHIPS = ("yl", "x")


def dot(subscripts, left, right):
    return jnp.einsum(subscripts, left, right, preferred_element_type=F32)


def swap(value):
    return lax.ppermute(value, "c", [(0, 1), (1, 0)])


def exchange(value, axis):
    return lax.all_to_all(value, axis, 0, 0)


def gather(value, axis, size):
    return exchange(jnp.broadcast_to(value[None], (size,) + value.shape), axis)


def split(value):
    high = value.astype(BF)
    return high, (value - high.astype(F32)).astype(BF)


def half(value, which, length, axis=0):
    return lax.dynamic_slice_in_dim(value, which * length, length, axis)


def shards(attention, output_projection, residual, gain, draft_weight, down, up, tenant_of, tenant_count):
    n_z, n_yh, n_yl, n_x, _ = SIZES
    n_chips = n_yl * n_x
    tenants = tenant_count.shape[0]
    rank = down.shape[1]
    tokens, block = residual.shape
    cols = output_projection.shape[1]
    out_block = draft_weight.shape[1]
    width = block * 2 * n_chips
    mine = tokens // 2
    core = lax.axis_index("c")
    chip = lax.axis_index(CHIPS)
    other = 1 - core
    first = core == 0

    yh = lax.axis_index("yh")
    turned = (yh - jnp.arange(n_yh, dtype=jnp.int32)) % n_yh

    def around(value):
        return [value] + [
            lax.ppermute(value, "yh", [(i, (i + s) % n_yh) for i in range(n_yh)]) for s in range(1, n_yh)
        ]

    def ordered(own, others):
        return jnp.where(first, own, others), jnp.where(first, others, own)

    upper = jnp.concatenate([up.T, jnp.zeros((rank, block - out_block), BF)], axis=1)
    joined = gather(jnp.concatenate([attention, down.T, upper], axis=0), "z", n_z)
    proj = jnp.concatenate(around(output_projection), axis=1)
    draft_weight_other = swap(draft_weight)
    pad = jnp.broadcast_to(gain[None], (16, block))
    kept = swap(jnp.concatenate([half(residual, other, mine), pad], axis=0))
    chip_rows = jnp.concatenate(
        ordered(jnp.concatenate([half(residual, core, mine), pad], axis=0), kept), axis=1
    )
    places = [(i, k) for i in range(n_z) for k in range(n_chips)]
    homes = [(i * n_chips + k, (i + k) % n_z * n_chips + k) for i, k in places]
    chips = [(i * n_chips + k, i * n_chips + (i - k) % n_chips) for i, k in places]
    chip_rows = lax.ppermute(chip_rows, ("z", "yl", "x"), chips)
    joined, chip_rows = lax.optimization_barrier((joined, chip_rows))
    residual_part, gain_part = chip_rows[:mine].astype(F32), chip_rows[mine : mine + 1].astype(F32)

    rows = n_z * mine
    z = lax.axis_index("z")
    order = (z + jnp.arange(n_z, dtype=jnp.int32)) % n_z
    send = half(joined[:, :tokens], other, mine, 1)[order].reshape(rows, block)
    keep = half(joined[:, :tokens], core, mine, 1)[order].reshape(rows, block)
    sent = swap(dot("tk,kn->tn", send, proj).astype(BF))
    pair = (dot("tk,kn->tn", keep, proj) + sent.astype(F32)).astype(BF)
    adapters = jnp.concatenate(
        [joined[:, tokens : tokens + rank], joined[:, tokens + rank :, :out_block]], axis=2
    ).reshape(n_z * rank, block + out_block)
    pair, adapters = lax.optimization_barrier((pair, adapters))
    parts = around(adapters)

    summed = jnp.sum(exchange(pair.reshape(n_chips, mine, n_yh * cols), CHIPS).astype(F32), axis=0).astype(BF)
    summed, parts[1], parts[3] = lax.optimization_barrier((summed, parts[1], parts[3]))
    summed = jnp.stack([summed[:, s * cols : (s + 1) * cols] for s in range(n_yh)])
    projected = lax.ppermute(summed[turned], ("z", "yl", "x"), homes)
    projected, parts[2] = lax.optimization_barrier((projected, parts[2]))

    hidden = residual_part + jnp.concatenate([projected[j] for j in range(n_yh)], axis=1).astype(F32)
    squares = jnp.sum(hidden * hidden, axis=1, keepdims=True)
    scaled = (hidden * gain_part).astype(BF)
    message = jnp.concatenate([scaled, *split(squares), jnp.zeros((mine, 126), BF)], axis=1)
    received = gather(message, CHIPS, n_chips)
    blocks = (z - jnp.arange(n_chips, dtype=jnp.int32)) % n_chips
    features = received[:, :, : 2 * block][blocks]
    totals = jnp.sum(received[:, :, 2 * block :].astype(F32), axis=0)
    inv_column = lax.rsqrt((totals[:, :1] + totals[:, 1:2]) / width + EPSILON)
    inv_row = jnp.broadcast_to(inv_column, (mine, 128)).T[:1]

    adapters_all = jnp.stack(parts)[turned].reshape(tenants * rank, block + out_block)
    adapters_other = swap(adapters_all)
    downs = jnp.concatenate(ordered(adapters_all[:, :block], adapters_other[:, :block]), axis=1)
    ups = jnp.concatenate([adapters_all[:, block:], adapters_other[:, block:]], axis=1)

    slot = jnp.arange(tenants * rank, dtype=jnp.int32) // rank
    slot_tenant = (slot % n_z) * n_yh + slot // n_z
    own_tenant = half(tenant_of, core, mine)
    partner_tenant = half(tenant_of, other, mine)
    own_mask = slot_tenant[:, None] == own_tenant[None, :]
    partner_mask = slot_tenant[:, None] == partner_tenant[None, :]

    def select(values):
        chosen = jnp.where(own_mask, values, 0.0)
        return jnp.sum(chosen.reshape(tenants, rank, mine), axis=0)

    def widen(values, mask):
        return jnp.where(mask, jnp.tile(values, (tenants, 1)), BF(0))

    chip_features = lax.dynamic_index_in_dim(features, chip, 0, keepdims=False)
    own_scaled = half(chip_features, core, block, 1)
    partner_scaled = swap(half(chip_features, other, block, 1))
    low_part = select(dot("jd,td->jt", downs, chip_features)) * inv_row

    target = lax.dynamic_slice(
        features, (chip // 2, 0, (chip % 2) * 2 * out_block), (1, mine, 2 * out_block)
    )[0]
    target = (target.astype(F32) * inv_column).astype(BF)
    next_row = swap(target[:16])[:1]
    target = jnp.concatenate([target[1:], next_row], axis=0)
    target = jnp.concatenate([half(target, core, out_block, 1), half(target, other, out_block, 1)], axis=1)

    following = jnp.roll(tenant_of, -1)
    position = jnp.arange(tokens, dtype=jnp.int32)
    keep_mask = (position < tokens - 1) & (tenant_of == following)
    is_tenant = tenant_of[:, None] == jnp.arange(tenants, dtype=jnp.int32)[None, :]
    count = jnp.sum(jnp.where(is_tenant, tenant_count.astype(F32)[None, :], 0.0), axis=1)
    weights = keep_mask.astype(F32) / count
    weight, weight_row = half(weights, core, mine)[:, None], half(weights, core, mine)[None]
    partner_weight, partner_weight_row = half(weights, other, mine)[:, None], half(weights, other, mine)[None]

    def plain(columns, part):
        draft = dot("ktd,kdn->tn", features, columns.reshape(n_chips, 2 * block, out_block))
        return (draft * inv_column - target[:, part * out_block : (part + 1) * out_block].astype(F32)) * weight

    plain_other = plain(draft_weight_other, 1).astype(BF)
    lanes = jnp.concatenate([*split(inv_column), jnp.zeros((mine, 126), BF)], axis=1)
    partner = swap(jnp.concatenate([plain_other, lanes], axis=1))
    plain_own = plain(draft_weight, 0)

    back_part = select(dot("jc,tc->jt", ups, jnp.concatenate([plain_own.astype(BF), plain_other], axis=1)))
    some = tenants * rank // 2
    some_ups = half(ups, core, some)
    same = slot[:some, None] == slot[None, :some]
    square_part = jnp.where(same, dot("jc,ic->ji", some_ups, some_ups), 0.0)
    square_part = jnp.sum(square_part.reshape(tenants // 2, rank, some), axis=0)
    codes = jnp.concatenate([low_part, back_part], axis=1)
    codes = gather(jnp.concatenate([*split(codes), square_part.astype(BF)], axis=1), MP, 2 * n_chips)
    codes = jnp.sum(codes.reshape(n_chips, 2, rank, 4 * mine + some).astype(F32), axis=0)
    square = jnp.concatenate([codes[0, :, 4 * mine :], codes[1, :, 4 * mine :]], axis=1).astype(BF)
    codes = codes[:, :, : 2 * mine] + codes[:, :, 2 * mine : 4 * mine]
    partner_inv = partner[:, out_block:].T
    partner_inv = partner_inv[:1].astype(F32) + partner_inv[1:2].astype(F32)

    def finish(code, mask, plain_grad, column, row, inv):
        low_wide = widen(code[:, :mine].astype(BF), mask)
        term = ADAPTER_SCALE * dot("jt,jn->tn", low_wide, ups[:, :out_block])
        grad = (plain_grad + term * column).astype(BF)
        back = code[:, mine:] + ADAPTER_SCALE * dot("rj,jt->rt", square, low_wide) * row
        return low_wide, grad, widen((ADAPTER_SCALE * back * inv).astype(BF), mask)

    low_wide, grad, back_wide = finish(
        half(codes, core, 1)[0], own_mask, plain_own, weight, weight_row, inv_row
    )
    partner_low, partner_grad, partner_back = finish(
        half(codes, other, 1)[0],
        partner_mask,
        partner[:, :out_block].astype(F32),
        partner_weight,
        partner_weight_row,
        partner_inv,
    )
    grad_up = dot("jt,tc->jc", low_wide, grad) + dot("jt,tc->jc", partner_low, partner_grad)
    grad_down = dot("jt,td->jd", back_wide, own_scaled) + dot("jt,td->jd", partner_back, partner_scaled)
    grads = jnp.concatenate([grad_down.astype(BF), grad_up.astype(BF)], axis=1)
    grads = exchange(grads.reshape(tenants, rank, block + out_block), ("yh", "z"))
    grads = jnp.sum(grads.astype(F32), axis=0)
    return grads[:, :block].T, grads[:, block:].T


def solution(mesh):
    split_mesh = Mesh(mesh.devices.reshape(SIZES), AXES)
    return jax.shard_map(
        shards,
        mesh=split_mesh,
        in_specs=(
            P(DP, MP),
            P(MP, DP),
            P(DP, MP),
            P(MP),
            P(None, MP),
            P(MP, DP),
            P(MP, DP),
            P(DP),
            P(),
        ),
        out_specs=(P(MP, DP), P(MP, DP)),
        check_vma=False,
    )
```

```python
import functools

import jax
import jax.numpy as jnp
from jax import lax
from jax.experimental import pallas as pl
from jax.experimental.pallas import tpu as pltpu
from jax.sharding import Mesh
from jax.sharding import PartitionSpec as P

EPSILON = 1e-06
ADAPTER_SCALE = 2.0
BF = jnp.bfloat16
F32 = jnp.float32

AXES = ("z", "yh", "yl", "x", "c")
SIZES = (8, 4, 2, 4, 2)
DP = ("z", "yh")
MP = ("yl", "x", "c")
CHIPS = ("yl", "x")


def dot(subscripts, left, right):
    return jnp.einsum(subscripts, left, right, preferred_element_type=F32)


def swap(value):
    return lax.ppermute(value, "c", [(0, 1), (1, 0)])


def exchange(value, axis):
    return lax.all_to_all(value, axis, 0, 0)


def gather(value, axis, size):
    return exchange(jnp.broadcast_to(value[None], (size,) + value.shape), axis)


def split(value):
    high = value.astype(BF)
    return high, (value - high.astype(F32)).astype(BF)


def half(value, which, length, axis=0):
    return lax.dynamic_slice_in_dim(value, which * length, length, axis)


def product_kernel(mine, place, joined, *refs):
    *pieces, out, rows = refs
    came = pieces.pop() if len(pieces) > 4 else None
    groups = joined.shape[0]
    start = pl.multiple_of(place[0] * mine, mine)
    for k in range(groups):
        rows[pl.ds(k * mine, mine), :] = joined[(place[1] + k) % groups, pl.ds(start, mine), :]
    cols = pieces[0].shape[1]
    for s, piece in enumerate(pieces):
        total = jnp.dot(rows[...], piece[...], preferred_element_type=F32)
        total = total.reshape(groups, mine, cols)
        lanes = pl.ds(s * cols, cols)
        if came is not None:
            total = total + came[:, :, lanes].astype(F32)
        out[:, :, lanes] = total.astype(BF)


def product(mine, which, z, joined, pieces, came=None):
    groups, depth = joined.shape[0], joined.shape[2]
    columns = sum(piece.shape[1] for piece in pieces)
    place = jnp.stack([which, z]).astype(jnp.int32)
    arrays = [joined, *pieces] + ([] if came is None else [came])
    vmem = pl.BlockSpec(memory_space=pltpu.VMEM)
    return pl.pallas_call(
        functools.partial(product_kernel, mine),
        out_shape=jax.ShapeDtypeStruct((groups, mine, columns), BF),
        in_specs=[pl.BlockSpec(memory_space=pltpu.SMEM)] + [vmem] * len(arrays),
        out_specs=vmem,
        scratch_shapes=[pltpu.VMEM((groups * mine, depth), BF)],
        compiler_params=pltpu.CompilerParams(vmem_limit_bytes=32 * 1024 * 1024),
        cost_estimate=pl.CostEstimate(
            flops=2 * groups * mine * depth * columns, bytes_accessed=4 * 1024 * 1024, transcendentals=0
        ),
    )(place, *arrays)


def shards(attention, output_projection, residual, gain, draft_weight, down, up, tenant_of, tenant_count):
    n_z, n_yh, n_yl, n_x, _ = SIZES
    n_chips = n_yl * n_x
    tenants = tenant_count.shape[0]
    rank = down.shape[1]
    tokens, block = residual.shape
    cols = output_projection.shape[1]
    out_block = draft_weight.shape[1]
    width = block * 2 * n_chips
    mine = tokens // 2
    core = lax.axis_index("c")
    chip = lax.axis_index(CHIPS)
    other = 1 - core
    first = core == 0

    yh = lax.axis_index("yh")
    turned = (yh - jnp.arange(n_yh, dtype=jnp.int32)) % n_yh

    def around(value):
        return [value] + [
            lax.ppermute(value, "yh", [(i, (i + s) % n_yh) for i in range(n_yh)]) for s in range(1, n_yh)
        ]

    def ordered(own, others):
        return jnp.where(first, own, others), jnp.where(first, others, own)

    upper = jnp.concatenate([up.T, jnp.zeros((rank, block - out_block), BF)], axis=1)
    joined = gather(jnp.concatenate([attention, down.T, upper], axis=0), "z", n_z)
    pieces = around(output_projection)
    draft_weight_other = swap(draft_weight)
    pad = jnp.broadcast_to(gain[None], (16, block))
    kept = swap(jnp.concatenate([half(residual, other, mine), pad], axis=0))
    chip_rows = jnp.concatenate(
        ordered(jnp.concatenate([half(residual, core, mine), pad], axis=0), kept), axis=1
    )
    places = [(i, k) for i in range(n_z) for k in range(n_chips)]
    homes = [(i * n_chips + k, (i + k) % n_z * n_chips + k) for i, k in places]
    chips = [(i * n_chips + k, i * n_chips + (i - k) % n_chips) for i, k in places]
    chip_rows = lax.ppermute(chip_rows, ("z", "yl", "x"), chips)
    joined, chip_rows = lax.optimization_barrier((joined, chip_rows))
    residual_part, gain_part = chip_rows[:mine].astype(F32), chip_rows[mine : mine + 1].astype(F32)

    z = lax.axis_index("z")
    sent = swap(product(mine, other, z, joined, pieces))
    pair = product(mine, core, z, joined, pieces, sent)
    adapters = jnp.concatenate(
        [joined[:, tokens : tokens + rank], joined[:, tokens + rank :, :out_block]], axis=2
    ).reshape(n_z * rank, block + out_block)
    pair, adapters = lax.optimization_barrier((pair, adapters))
    parts = around(adapters)

    summed = jnp.sum(exchange(pair, CHIPS).astype(F32), axis=0).astype(BF)
    summed = jnp.stack([summed[:, s * cols : (s + 1) * cols] for s in range(n_yh)])
    projected = lax.ppermute(summed[turned], ("z", "yl", "x"), homes)
    projected, *parts = lax.optimization_barrier((projected, *parts))

    hidden = residual_part + jnp.concatenate([projected[j] for j in range(n_yh)], axis=1).astype(F32)
    squares = jnp.sum(hidden * hidden, axis=1, keepdims=True)
    scaled = (hidden * gain_part).astype(BF)
    message = jnp.concatenate([scaled, *split(squares), jnp.zeros((mine, 126), BF)], axis=1)
    received = gather(message, CHIPS, n_chips)
    blocks = (z - jnp.arange(n_chips, dtype=jnp.int32)) % n_chips
    features = received[:, :, : 2 * block][blocks]
    totals = jnp.sum(received[:, :, 2 * block :].astype(F32), axis=0)
    inv_column = lax.rsqrt((totals[:, :1] + totals[:, 1:2]) / width + EPSILON)
    inv_row = jnp.broadcast_to(inv_column, (mine, 128)).T[:1]

    adapters_all = jnp.stack(parts)[turned].reshape(tenants * rank, block + out_block)
    adapters_other = swap(adapters_all)
    downs = jnp.concatenate(ordered(adapters_all[:, :block], adapters_other[:, :block]), axis=1)
    ups = jnp.concatenate([adapters_all[:, block:], adapters_other[:, block:]], axis=1)

    slot = jnp.arange(tenants * rank, dtype=jnp.int32) // rank
    slot_tenant = (slot % n_z) * n_yh + slot // n_z
    own_tenant = half(tenant_of, core, mine)
    partner_tenant = half(tenant_of, other, mine)
    own_mask = slot_tenant[:, None] == own_tenant[None, :]
    partner_mask = slot_tenant[:, None] == partner_tenant[None, :]

    def select(values):
        chosen = jnp.where(own_mask, values, 0.0)
        return jnp.sum(chosen.reshape(tenants, rank, mine), axis=0)

    def widen(values, mask):
        return jnp.where(mask, jnp.tile(values, (tenants, 1)), BF(0))

    chip_features = lax.dynamic_index_in_dim(features, chip, 0, keepdims=False)
    own_scaled = half(chip_features, core, block, 1)
    low_part = select(dot("jd,td->jt", downs, chip_features)) * inv_row

    target = lax.dynamic_slice(
        features, (chip // 2, 0, (chip % 2) * 2 * out_block), (1, mine, 2 * out_block)
    )[0]
    target = (target.astype(F32) * inv_column).astype(BF)
    came = swap(jnp.concatenate([half(chip_features, other, block, 1), target[:16]], axis=0))
    partner_scaled, next_row = came[:mine], came[mine : mine + 1]
    target = jnp.concatenate([target[1:], next_row], axis=0)
    target = jnp.concatenate([half(target, core, out_block, 1), half(target, other, out_block, 1)], axis=1)

    following = jnp.roll(tenant_of, -1)
    position = jnp.arange(tokens, dtype=jnp.int32)
    keep_mask = (position < tokens - 1) & (tenant_of == following)
    is_tenant = tenant_of[:, None] == jnp.arange(tenants, dtype=jnp.int32)[None, :]
    count = jnp.sum(jnp.where(is_tenant, tenant_count.astype(F32)[None, :], 0.0), axis=1)
    weights = keep_mask.astype(F32) / count
    weight, weight_row = half(weights, core, mine)[:, None], half(weights, core, mine)[None]
    partner_weight, partner_weight_row = half(weights, other, mine)[:, None], half(weights, other, mine)[None]

    def plain(columns, part):
        draft = dot("ktd,kdn->tn", features, columns.reshape(n_chips, 2 * block, out_block))
        return (draft * inv_column - target[:, part * out_block : (part + 1) * out_block].astype(F32)) * weight

    plain_other = plain(draft_weight_other, 1).astype(BF)
    lanes = jnp.concatenate([*split(inv_column), jnp.zeros((mine, 126), BF)], axis=1)
    partner = swap(jnp.concatenate([plain_other, lanes], axis=1))
    plain_own = plain(draft_weight, 0)

    back_part = select(dot("jc,tc->jt", ups, jnp.concatenate([plain_own.astype(BF), plain_other], axis=1)))
    some = tenants * rank // 2
    some_ups = half(ups, core, some)
    same = slot[:some, None] == slot[None, :some]
    square_part = jnp.where(same, dot("jc,ic->ji", some_ups, some_ups), 0.0)
    square_part = jnp.sum(square_part.reshape(tenants // 2, rank, some), axis=0)
    codes = jnp.concatenate([low_part, back_part], axis=1)
    codes = gather(jnp.concatenate([*split(codes), square_part.astype(BF)], axis=1), MP, 2 * n_chips)
    codes = jnp.sum(codes.reshape(n_chips, 2, rank, 4 * mine + some).astype(F32), axis=0)
    square = jnp.concatenate([codes[0, :, 4 * mine :], codes[1, :, 4 * mine :]], axis=1).astype(BF)
    codes = codes[:, :, : 2 * mine] + codes[:, :, 2 * mine : 4 * mine]
    partner_inv = partner[:, out_block:].T
    partner_inv = partner_inv[:1].astype(F32) + partner_inv[1:2].astype(F32)

    def finish(code, mask, plain_grad, column, row, inv):
        low_wide = widen(code[:, :mine].astype(BF), mask)
        term = ADAPTER_SCALE * dot("jt,jn->tn", low_wide, ups[:, :out_block])
        grad = (plain_grad + term * column).astype(BF)
        back = code[:, mine:] + ADAPTER_SCALE * dot("rj,jt->rt", square, low_wide) * row
        return low_wide, grad, widen((ADAPTER_SCALE * back * inv).astype(BF), mask)

    low_wide, grad, back_wide = finish(
        half(codes, core, 1)[0], own_mask, plain_own, weight, weight_row, inv_row
    )
    partner_low, partner_grad, partner_back = finish(
        half(codes, other, 1)[0],
        partner_mask,
        partner[:, :out_block].astype(F32),
        partner_weight,
        partner_weight_row,
        partner_inv,
    )
    grad_up = dot("jt,tc->jc", low_wide, grad) + dot("jt,tc->jc", partner_low, partner_grad)
    grad_down = dot("jt,td->jd", back_wide, own_scaled) + dot("jt,td->jd", partner_back, partner_scaled)
    grads = jnp.concatenate([grad_down.astype(BF), grad_up.astype(BF)], axis=1)
    grads = exchange(grads.reshape(tenants, rank, block + out_block), ("yh", "z"))
    grads = jnp.sum(grads.astype(F32), axis=0)
    return grads[:, :block].T, grads[:, block:].T


def solution(mesh):
    split_mesh = Mesh(mesh.devices.reshape(SIZES), AXES)
    return jax.shard_map(
        shards,
        mesh=split_mesh,
        in_specs=(
            P(DP, MP),
            P(MP, DP),
            P(DP, MP),
            P(MP),
            P(None, MP),
            P(MP, DP),
            P(MP, DP),
            P(DP),
            P(),
        ),
        out_specs=(P(MP, DP), P(MP, DP)),
        check_vma=False,
    )
```

```python
import functools

import jax
import jax.numpy as jnp
from jax import lax
from jax.experimental import pallas as pl
from jax.experimental.pallas import tpu as pltpu
from jax.sharding import Mesh
from jax.sharding import PartitionSpec as P

EPSILON = 1e-06
ADAPTER_SCALE = 2.0
BF = jnp.bfloat16
F32 = jnp.float32

AXES = ("z", "yh", "yl", "x", "c")
SIZES = (8, 4, 2, 4, 2)
DP = ("z", "yh")
MP = ("yl", "x", "c")
CHIPS = ("yl", "x")


def dot(subscripts, left, right):
    return jnp.einsum(subscripts, left, right, preferred_element_type=F32)


def swap(value):
    return lax.ppermute(value, "c", [(0, 1), (1, 0)])


def exchange(value, axis):
    return lax.all_to_all(value, axis, 0, 0)


def gather(value, axis, size):
    return exchange(jnp.broadcast_to(value[None], (size,) + value.shape), axis)


def split(value):
    high = value.astype(BF)
    return high, (value - high.astype(F32)).astype(BF)


def half(value, which, length, axis=0):
    return lax.dynamic_slice_in_dim(value, which * length, length, axis)


def product_kernel(mine, place, joined, *refs):
    *pieces, out, rows = refs
    came = pieces.pop() if len(pieces) > 4 else None
    groups = joined.shape[0]
    start = pl.multiple_of(place[0] * mine, mine)
    for k in range(groups):
        rows[pl.ds(k * mine, mine), :] = joined[(place[1] + k) % groups, pl.ds(start, mine), :]
    cols = pieces[0].shape[1]
    for s, piece in enumerate(pieces):
        total = jnp.dot(rows[...], piece[...], preferred_element_type=F32)
        total = total.reshape(groups, mine, cols)
        lanes = pl.ds(s * cols, cols)
        if came is not None:
            total = total + came[:, :, lanes].astype(F32)
        out[:, :, lanes] = total.astype(BF)


def product(mine, which, z, joined, pieces, came=None):
    groups, depth = joined.shape[0], joined.shape[2]
    columns = sum(piece.shape[1] for piece in pieces)
    place = jnp.stack([which, z]).astype(jnp.int32)
    arrays = [joined, *pieces] + ([] if came is None else [came])
    vmem = pl.BlockSpec(memory_space=pltpu.VMEM)
    return pl.pallas_call(
        functools.partial(product_kernel, mine),
        out_shape=jax.ShapeDtypeStruct((groups, mine, columns), BF),
        in_specs=[pl.BlockSpec(memory_space=pltpu.SMEM)] + [vmem] * len(arrays),
        out_specs=vmem,
        scratch_shapes=[pltpu.VMEM((groups * mine, depth), BF)],
        compiler_params=pltpu.CompilerParams(vmem_limit_bytes=32 * 1024 * 1024),
        cost_estimate=pl.CostEstimate(
            flops=2 * groups * mine * depth * columns, bytes_accessed=4 * 1024 * 1024, transcendentals=0
        ),
    )(place, *arrays)


def shards(attention, output_projection, residual, gain, draft_weight, down, up, tenant_of, tenant_count):
    n_z, n_yh, n_yl, n_x, _ = SIZES
    n_chips = n_yl * n_x
    tenants = tenant_count.shape[0]
    rank = down.shape[1]
    tokens, block = residual.shape
    cols = output_projection.shape[1]
    out_block = draft_weight.shape[1]
    width = block * 2 * n_chips
    mine = tokens // 2
    core = lax.axis_index("c")
    chip = lax.axis_index(CHIPS)
    other = 1 - core
    first = core == 0

    yh = lax.axis_index("yh")
    turned = (yh - jnp.arange(n_yh, dtype=jnp.int32)) % n_yh

    def shift(value, step):
        return lax.ppermute(value, "yh", [(i, (i + step) % n_yh) for i in range(n_yh)])

    def ordered(own, others):
        return jnp.where(first, own, others), jnp.where(first, others, own)

    upper = jnp.concatenate([up.T, jnp.zeros((rank, block - out_block), BF)], axis=1)
    joined = gather(jnp.concatenate([attention, down.T, upper], axis=0), "z", n_z)
    pieces = [output_projection] + [shift(output_projection, step) for step in range(1, n_yh)]
    draft_weight_other = swap(draft_weight)
    pad = jnp.broadcast_to(gain[None], (16, block))
    kept = swap(jnp.concatenate([half(residual, other, mine), pad], axis=0))
    chip_rows = jnp.concatenate(
        ordered(jnp.concatenate([half(residual, core, mine), pad], axis=0), kept), axis=1
    )
    places = [(i, k) for i in range(n_z) for k in range(n_chips)]
    homes = [(i * n_chips + k, (i + k) % n_z * n_chips + k) for i, k in places]
    chips = [(i * n_chips + k, i * n_chips + (i - k) % n_chips) for i, k in places]
    chip_rows = lax.ppermute(chip_rows, ("z", "yl", "x"), chips)
    slot = jnp.arange(tenants * rank, dtype=jnp.int32) // rank
    slot_tenant = (slot % n_z) * n_yh + slot // n_z
    own_tenant = half(tenant_of, core, mine)
    partner_tenant = half(tenant_of, other, mine)
    own_mask = slot_tenant[:, None] == own_tenant[None, :]
    partner_mask = slot_tenant[:, None] == partner_tenant[None, :]
    following = jnp.roll(tenant_of, -1)
    position = jnp.arange(tokens, dtype=jnp.int32)
    keep_mask = (position < tokens - 1) & (tenant_of == following)
    is_tenant = tenant_of[:, None] == jnp.arange(tenants, dtype=jnp.int32)[None, :]
    count = jnp.sum(jnp.where(is_tenant, tenant_count.astype(F32)[None, :], 0.0), axis=1)
    weights = keep_mask.astype(F32) / count
    joined, chip_rows, draft_weight_other, own_mask, partner_mask, weights = lax.optimization_barrier(
        (joined, chip_rows, draft_weight_other, own_mask, partner_mask, weights)
    )
    residual_part, gain_part = chip_rows[:mine].astype(F32), chip_rows[mine : mine + 1].astype(F32)

    z = lax.axis_index("z")
    sent = swap(product(mine, other, z, joined, pieces))
    pair = product(mine, core, z, joined, pieces, sent)
    adapters = jnp.concatenate(
        [joined[:, tokens : tokens + rank], joined[:, tokens + rank :, :out_block]], axis=2
    ).reshape(n_z * rank, block + out_block)
    pair, adapters = lax.optimization_barrier((pair, adapters))
    before, after = shift(adapters, 1), shift(adapters, -1)

    summed = jnp.sum(exchange(pair, CHIPS).astype(F32), axis=0).astype(BF)
    summed, before, after, adapters = lax.optimization_barrier((summed, before, after, adapters))
    some = n_z * rank // 2
    parts = [adapters, before, jnp.concatenate([shift(adapters[:some], 2), shift(after[some:], -1)], axis=0), after]
    summed = jnp.stack([summed[:, s * cols : (s + 1) * cols] for s in range(n_yh)])
    projected = lax.ppermute(summed[turned], ("z", "yl", "x"), homes)

    hidden = residual_part + jnp.concatenate([projected[j] for j in range(n_yh)], axis=1).astype(F32)
    squares = jnp.sum(hidden * hidden, axis=1, keepdims=True)
    scaled = (hidden * gain_part).astype(BF)
    message = jnp.concatenate([scaled, *split(squares), jnp.zeros((mine, 126), BF)], axis=1)
    received = gather(message, CHIPS, n_chips)
    blocks = (z - jnp.arange(n_chips, dtype=jnp.int32)) % n_chips
    features = received[:, :, : 2 * block][blocks]
    totals = jnp.sum(received[:, :, 2 * block :].astype(F32), axis=0)
    inv_column = lax.rsqrt((totals[:, :1] + totals[:, 1:2]) / width + EPSILON)
    inv_row = jnp.broadcast_to(inv_column, (mine, 128)).T[:1]

    _, later = lax.optimization_barrier((message, turned))
    adapters_all = jnp.stack(parts)[later].reshape(tenants * rank, block + out_block)
    adapters_other = swap(adapters_all)
    downs = jnp.concatenate(ordered(adapters_all[:, :block], adapters_other[:, :block]), axis=1)
    ups = jnp.concatenate([adapters_all[:, block:], adapters_other[:, block:]], axis=1)

    def select(values):
        chosen = jnp.where(own_mask, values, 0.0)
        return jnp.sum(chosen.reshape(tenants, rank, mine), axis=0)

    def widen(values, mask):
        return jnp.where(mask, jnp.tile(values, (tenants, 1)), BF(0))

    chip_features = lax.dynamic_index_in_dim(features, chip, 0, keepdims=False)
    own_scaled = half(chip_features, core, block, 1)
    low_part = select(dot("jd,td->jt", downs, chip_features)) * inv_row

    target = lax.dynamic_slice(
        features, (chip // 2, 0, (chip % 2) * 2 * out_block), (1, mine, 2 * out_block)
    )[0]
    target = (target.astype(F32) * inv_column).astype(BF)
    came = swap(jnp.concatenate([half(chip_features, other, block, 1), target[:16]], axis=0))
    partner_scaled, next_row = came[:mine], came[mine : mine + 1]
    target = jnp.concatenate([target[1:], next_row], axis=0)
    target = jnp.concatenate([half(target, core, out_block, 1), half(target, other, out_block, 1)], axis=1)

    weight, weight_row = half(weights, core, mine)[:, None], half(weights, core, mine)[None]
    partner_weight, partner_weight_row = half(weights, other, mine)[:, None], half(weights, other, mine)[None]

    def plain(columns, part):
        draft = dot("ktd,kdn->tn", features, columns.reshape(n_chips, 2 * block, out_block))
        return (draft * inv_column - target[:, part * out_block : (part + 1) * out_block].astype(F32)) * weight

    plain_other = plain(draft_weight_other, 1).astype(BF)
    lanes = jnp.concatenate([*split(inv_column), jnp.zeros((mine, 126), BF)], axis=1)
    partner = swap(jnp.concatenate([plain_other, lanes], axis=1))
    plain_own = plain(draft_weight, 0)

    back_part = select(dot("jc,tc->jt", ups, jnp.concatenate([plain_own.astype(BF), plain_other], axis=1)))
    some = tenants * rank // 2
    some_ups = half(ups, core, some)
    same = slot[:some, None] == slot[None, :some]
    square_part = jnp.where(same, dot("jc,ic->ji", some_ups, some_ups), 0.0)
    square_part = jnp.sum(square_part.reshape(tenants // 2, rank, some), axis=0)
    codes = jnp.concatenate([low_part, back_part], axis=1)
    codes = gather(jnp.concatenate([*split(codes), square_part.astype(BF)], axis=1), MP, 2 * n_chips)
    codes = jnp.sum(codes.reshape(n_chips, 2, rank, 4 * mine + some).astype(F32), axis=0)
    square = jnp.concatenate([codes[0, :, 4 * mine :], codes[1, :, 4 * mine :]], axis=1).astype(BF)
    codes = codes[:, :, : 2 * mine] + codes[:, :, 2 * mine : 4 * mine]
    partner_inv = partner[:, out_block:].T
    partner_inv = partner_inv[:1].astype(F32) + partner_inv[1:2].astype(F32)

    def finish(code, mask, plain_grad, column, row, inv):
        low_wide = widen(code[:, :mine].astype(BF), mask)
        term = ADAPTER_SCALE * dot("jt,jn->tn", low_wide, ups[:, :out_block])
        grad = (plain_grad + term * column).astype(BF)
        back = code[:, mine:] + ADAPTER_SCALE * dot("rj,jt->rt", square, low_wide) * row
        return low_wide, grad, widen((ADAPTER_SCALE * back * inv).astype(BF), mask)

    low_wide, grad, back_wide = finish(
        half(codes, core, 1)[0], own_mask, plain_own, weight, weight_row, inv_row
    )
    partner_low, partner_grad, partner_back = finish(
        half(codes, other, 1)[0],
        partner_mask,
        partner[:, :out_block].astype(F32),
        partner_weight,
        partner_weight_row,
        partner_inv,
    )
    grad_up = dot("jt,tc->jc", low_wide, grad) + dot("jt,tc->jc", partner_low, partner_grad)
    grad_down = dot("jt,td->jd", back_wide, own_scaled) + dot("jt,td->jd", partner_back, partner_scaled)
    grads = jnp.concatenate([grad_down.astype(BF), grad_up.astype(BF)], axis=1)
    grads = exchange(grads.reshape(tenants, rank, block + out_block), ("yh", "z"))
    grads = jnp.sum(grads.astype(F32), axis=0)
    return grads[:, :block].T, grads[:, block:].T


def solution(mesh):
    split_mesh = Mesh(mesh.devices.reshape(SIZES), AXES)
    return jax.shard_map(
        shards,
        mesh=split_mesh,
        in_specs=(
            P(DP, MP),
            P(MP, DP),
            P(DP, MP),
            P(MP),
            P(None, MP),
            P(MP, DP),
            P(MP, DP),
            P(DP),
            P(),
        ),
        out_specs=(P(MP, DP), P(MP, DP)),
        check_vma=False,
    )
```

```python
import functools

import jax
import jax.numpy as jnp
from jax import lax
from jax.experimental import pallas as pl
from jax.experimental.pallas import tpu as pltpu
from jax.sharding import Mesh
from jax.sharding import PartitionSpec as P

EPSILON = 1e-06
ADAPTER_SCALE = 2.0
BF = jnp.bfloat16
F32 = jnp.float32

AXES = ("z", "yh", "yl", "x", "c")
SIZES = (8, 4, 2, 4, 2)
DP = ("z", "yh")
MP = ("yl", "x", "c")
CHIPS = ("yl", "x")


def dot(subscripts, left, right):
    return jnp.einsum(subscripts, left, right, preferred_element_type=F32)


def swap(value):
    return lax.ppermute(value, "c", [(0, 1), (1, 0)])


def exchange(value, axis):
    return lax.all_to_all(value, axis, 0, 0)


def gather(value, axis, size):
    return exchange(jnp.broadcast_to(value[None], (size,) + value.shape), axis)


def split(value):
    high = value.astype(BF)
    return high, (value - high.astype(F32)).astype(BF)


def half(value, which, length, axis=0):
    return lax.dynamic_slice_in_dim(value, which * length, length, axis)


def product_kernel(mine, place, joined, *refs):
    *pieces, out, rows = refs
    came = pieces.pop() if len(pieces) > 4 else None
    groups = joined.shape[0]
    start = pl.multiple_of(place[0] * mine, mine)
    for k in range(groups):
        rows[pl.ds(k * mine, mine), :] = joined[(place[1] + k) % groups, pl.ds(start, mine), :]
    cols = pieces[0].shape[1]
    for s, piece in enumerate(pieces):
        total = jnp.dot(rows[...], piece[...], preferred_element_type=F32)
        total = total.reshape(groups, mine, cols)
        lanes = pl.ds(s * cols, cols)
        if came is not None:
            total = total + came[:, :, lanes].astype(F32)
        out[:, :, lanes] = total.astype(BF)


def product(mine, which, z, joined, pieces, came=None):
    groups, depth = joined.shape[0], joined.shape[2]
    columns = sum(piece.shape[1] for piece in pieces)
    place = jnp.stack([which, z]).astype(jnp.int32)
    arrays = [joined, *pieces] + ([] if came is None else [came])
    vmem = pl.BlockSpec(memory_space=pltpu.VMEM)
    return pl.pallas_call(
        functools.partial(product_kernel, mine),
        out_shape=jax.ShapeDtypeStruct((groups, mine, columns), BF),
        in_specs=[pl.BlockSpec(memory_space=pltpu.SMEM)] + [vmem] * len(arrays),
        out_specs=vmem,
        scratch_shapes=[pltpu.VMEM((groups * mine, depth), BF)],
        compiler_params=pltpu.CompilerParams(vmem_limit_bytes=32 * 1024 * 1024),
        cost_estimate=pl.CostEstimate(
            flops=2 * groups * mine * depth * columns, bytes_accessed=4 * 1024 * 1024, transcendentals=0
        ),
    )(place, *arrays)


def shards(attention, output_projection, residual, gain, draft_weight, down, up, tenant_of, tenant_count):
    n_z, n_yh, n_yl, n_x, _ = SIZES
    n_chips = n_yl * n_x
    tenants = tenant_count.shape[0]
    rank = down.shape[1]
    tokens, block = residual.shape
    cols = output_projection.shape[1]
    out_block = draft_weight.shape[1]
    width = block * 2 * n_chips
    mine = tokens // 2
    core = lax.axis_index("c")
    chip = lax.axis_index(CHIPS)
    other = 1 - core
    first = core == 0

    yh = lax.axis_index("yh")
    turned = (yh - jnp.arange(n_yh, dtype=jnp.int32)) % n_yh

    def around(value):
        return [value] + [
            lax.ppermute(value, "yh", [(i, (i + s) % n_yh) for i in range(n_yh)]) for s in range(1, n_yh)
        ]

    def ordered(own, others):
        return jnp.where(first, own, others), jnp.where(first, others, own)

    upper = jnp.concatenate([up.T, jnp.zeros((rank, block - out_block), BF)], axis=1)
    joined = jnp.concatenate(
        [jnp.broadcast_to(part[None], (n_z,) + part.shape) for part in (attention, down.T, upper)], axis=1
    )
    joined = exchange(joined, "z")
    pieces = around(output_projection)
    draft_weight_other = swap(draft_weight)
    pad = jnp.broadcast_to(gain[None], (16, block))
    kept = swap(jnp.concatenate([half(residual, other, mine), pad], axis=0))
    chip_rows = jnp.concatenate(
        ordered(jnp.concatenate([half(residual, core, mine), pad], axis=0), kept), axis=1
    )
    places = [(i, k) for i in range(n_z) for k in range(n_chips)]
    homes = [(i * n_chips + k, (i + k) % n_z * n_chips + k) for i, k in places]
    chips = [(i * n_chips + k, i * n_chips + (i - k) % n_chips) for i, k in places]
    chip_rows = lax.ppermute(chip_rows, ("z", "yl", "x"), chips)
    slot = jnp.arange(tenants * rank, dtype=jnp.int32) // rank
    slot_tenant = (slot % n_z) * n_yh + slot // n_z
    own_tenant = half(tenant_of, core, mine)
    partner_tenant = half(tenant_of, other, mine)
    own_mask = slot_tenant[:, None] == own_tenant[None, :]
    partner_mask = slot_tenant[:, None] == partner_tenant[None, :]
    following = jnp.roll(tenant_of, -1)
    position = jnp.arange(tokens, dtype=jnp.int32)
    keep_mask = (position < tokens - 1) & (tenant_of == following)
    is_tenant = tenant_of[:, None] == jnp.arange(tenants, dtype=jnp.int32)[None, :]
    count = jnp.sum(jnp.where(is_tenant, tenant_count.astype(F32)[None, :], 0.0), axis=1)
    weights = keep_mask.astype(F32) / count
    joined, chip_rows, own_mask, partner_mask, weights = lax.optimization_barrier(
        (joined, chip_rows, own_mask, partner_mask, weights)
    )
    residual_part, gain_part = chip_rows[:mine].astype(F32), chip_rows[mine : mine + 1].astype(F32)

    z = lax.axis_index("z")
    sent = swap(product(mine, other, z, joined, pieces))
    pair = product(mine, core, z, joined, pieces, sent)
    adapters = jnp.concatenate(
        [joined[:, tokens : tokens + rank], joined[:, tokens + rank :, :out_block]], axis=2
    ).reshape(n_z * rank, block + out_block)
    pair, adapters = lax.optimization_barrier((pair, adapters))
    parts = around(adapters)

    summed = jnp.sum(exchange(pair, CHIPS).astype(F32), axis=0).astype(BF)
    summed = jnp.stack([summed[:, s * cols : (s + 1) * cols] for s in range(n_yh)])
    projected = lax.ppermute(summed[turned], ("z", "yl", "x"), homes)
    projected, *parts = lax.optimization_barrier((projected, *parts))

    hidden = residual_part + jnp.concatenate([projected[j] for j in range(n_yh)], axis=1).astype(F32)
    squares = jnp.sum(hidden * hidden, axis=1, keepdims=True)
    scaled = (hidden * gain_part).astype(BF)
    message = jnp.concatenate([scaled, *split(squares), jnp.zeros((mine, 126), BF)], axis=1)
    received = gather(message, CHIPS, n_chips)
    blocks = (z - jnp.arange(n_chips, dtype=jnp.int32)) % n_chips
    features = received[:, :, : 2 * block][blocks]
    totals = jnp.sum(received[:, :, 2 * block :].astype(F32), axis=0)
    inv_column = lax.rsqrt((totals[:, :1] + totals[:, 1:2]) / width + EPSILON)
    inv_row = jnp.broadcast_to(inv_column, (mine, 128)).T[:1]

    adapters_all = jnp.stack(parts)[turned].reshape(tenants * rank, block + out_block)
    downs, ups = adapters_all[:, :block], adapters_all[:, block:]

    def select(values, mask):
        chosen = jnp.where(mask, values, 0.0)
        return jnp.sum(chosen.reshape(tenants, rank, mine), axis=0)

    def widen(values, mask):
        return jnp.where(mask, jnp.tile(values, (tenants, 1)), BF(0))

    chip_features = lax.dynamic_index_in_dim(features, chip, 0, keepdims=False)
    own_scaled = half(chip_features, core, block, 1)
    target = lax.dynamic_slice(
        features, (chip // 2, 0, (chip % 2) * 2 * out_block), (1, mine, 2 * out_block)
    )[0]
    target = (target.astype(F32) * inv_column).astype(BF)
    came = swap(jnp.concatenate([half(chip_features, other, block, 1), target[:16]], axis=0))
    partner_scaled, next_row = came[:mine], came[mine : mine + 1]
    low_parts = ordered(
        select(dot("jd,td->jt", downs, own_scaled), own_mask),
        select(dot("jd,td->jt", downs, partner_scaled), partner_mask),
    )
    target = jnp.concatenate([target[1:], next_row], axis=0)
    target = jnp.concatenate([half(target, core, out_block, 1), half(target, other, out_block, 1)], axis=1)

    weight, weight_row = half(weights, core, mine)[:, None], half(weights, core, mine)[None]
    partner_weight, partner_weight_row = half(weights, other, mine)[:, None], half(weights, other, mine)[None]

    def plain(columns, part):
        draft = dot("ktd,kdn->tn", features, columns.reshape(n_chips, 2 * block, out_block))
        return (draft * inv_column - target[:, part * out_block : (part + 1) * out_block].astype(F32)) * weight

    plain_other = plain(draft_weight_other, 1).astype(BF)
    lanes = jnp.concatenate([*split(inv_column), jnp.zeros((mine, 126), BF)], axis=1)
    partner = swap(jnp.concatenate([plain_other, lanes], axis=1))
    plain_own = plain(draft_weight, 0)

    back_parts = ordered(
        select(dot("jc,tc->jt", ups, plain_own.astype(BF)), own_mask),
        select(dot("jc,tc->jt", ups, partner[:, :out_block]), partner_mask),
    )
    square = jnp.where(slot[:, None] == slot[None, :], dot("jc,ic->ji", ups, ups), 0.0)
    square = jnp.sum(square.reshape(tenants, rank, tenants * rank), axis=0)
    codes = jnp.concatenate([*low_parts, *back_parts, square], axis=1).astype(BF)
    codes = jnp.sum(gather(codes, MP, 2 * n_chips).astype(F32), axis=0)
    square = codes[:, 4 * mine :].astype(BF)
    lows = ordered(codes[:, :mine], codes[:, mine : 2 * mine])
    backs = ordered(codes[:, 2 * mine : 3 * mine], codes[:, 3 * mine : 4 * mine])
    partner_inv = partner[:, out_block:].T
    partner_inv = partner_inv[:1].astype(F32) + partner_inv[1:2].astype(F32)

    def finish(low, back, mask, plain_grad, column, row, inv):
        low_wide = widen((low * inv).astype(BF), mask)
        term = ADAPTER_SCALE * dot("jt,jn->tn", low_wide, ups)
        grad = (plain_grad + term * column).astype(BF)
        back = back + ADAPTER_SCALE * dot("rj,jt->rt", square, low_wide) * row
        return low_wide, grad, widen((ADAPTER_SCALE * back * inv).astype(BF), mask)

    low_wide, grad, back_wide = finish(
        lows[0], backs[0], own_mask, plain_own, weight, weight_row, inv_row
    )
    partner_low, partner_grad, partner_back = finish(
        lows[1],
        backs[1],
        partner_mask,
        partner[:, :out_block].astype(F32),
        partner_weight,
        partner_weight_row,
        partner_inv,
    )
    grad_up = dot("jt,tc->jc", low_wide, grad) + dot("jt,tc->jc", partner_low, partner_grad)
    grad_down = dot("jt,td->jd", back_wide, own_scaled) + dot("jt,td->jd", partner_back, partner_scaled)
    grads = jnp.concatenate([grad_down.astype(BF), grad_up.astype(BF)], axis=1)
    grads = exchange(grads.reshape(tenants, rank, block + out_block), ("yh", "z"))
    grads = jnp.sum(grads.astype(F32), axis=0)
    return grads[:, :block].T, grads[:, block:].T


def solution(mesh):
    split_mesh = Mesh(mesh.devices.reshape(SIZES), AXES)
    return jax.shard_map(
        shards,
        mesh=split_mesh,
        in_specs=(
            P(DP, MP),
            P(MP, DP),
            P(DP, MP),
            P(MP),
            P(None, MP),
            P(MP, DP),
            P(MP, DP),
            P(DP),
            P(),
        ),
        out_specs=(P(MP, DP), P(MP, DP)),
        check_vma=False,
    )
```

```python
import functools

import jax
import jax.numpy as jnp
from jax import lax
from jax.experimental import pallas as pl
from jax.experimental.pallas import tpu as pltpu
from jax.sharding import Mesh
from jax.sharding import PartitionSpec as P

EPSILON = 1e-06
ADAPTER_SCALE = 2.0
BF = jnp.bfloat16
F32 = jnp.float32

AXES = ("z", "yh", "yl", "x", "c")
SIZES = (8, 4, 2, 4, 2)
DP = ("z", "yh")
MP = ("yl", "x", "c")
CHIPS = ("yl", "x")


def dot(subscripts, left, right):
    return jnp.einsum(subscripts, left, right, preferred_element_type=F32)


def swap(value):
    return lax.ppermute(value, "c", [(0, 1), (1, 0)])


def exchange(value, axis):
    return lax.all_to_all(value, axis, 0, 0)


def gather(value, axis, size):
    return exchange(jnp.broadcast_to(value[None], (size,) + value.shape), axis)


def split(value):
    high = value.astype(BF)
    return high, (value - high.astype(F32)).astype(BF)


def half(value, which, length, axis=0):
    return lax.dynamic_slice_in_dim(value, which * length, length, axis)


def product_kernel(mine, place, joined, *refs):
    *pieces, out, rows = refs
    came = pieces.pop() if len(pieces) > 4 else None
    groups = joined.shape[0]
    start = pl.multiple_of(place[0] * mine, mine)
    for k in range(groups):
        rows[pl.ds(k * mine, mine), :] = joined[(place[1] + k) % groups, pl.ds(start, mine), :]
    cols = pieces[0].shape[1]
    for s, piece in enumerate(pieces):
        total = jnp.dot(rows[...], piece[...], preferred_element_type=F32)
        total = total.reshape(groups, mine, cols)
        lanes = pl.ds(s * cols, cols)
        if came is not None:
            total = total + came[:, :, lanes].astype(F32)
        out[:, :, lanes] = total.astype(BF)


def product(mine, which, z, joined, pieces, came=None):
    groups, depth = joined.shape[0], joined.shape[2]
    columns = sum(piece.shape[1] for piece in pieces)
    place = jnp.stack([which, z]).astype(jnp.int32)
    arrays = [joined, *pieces] + ([] if came is None else [came])
    vmem = pl.BlockSpec(memory_space=pltpu.VMEM)
    return pl.pallas_call(
        functools.partial(product_kernel, mine),
        out_shape=jax.ShapeDtypeStruct((groups, mine, columns), BF),
        in_specs=[pl.BlockSpec(memory_space=pltpu.SMEM)] + [vmem] * len(arrays),
        out_specs=vmem,
        scratch_shapes=[pltpu.VMEM((groups * mine, depth), BF)],
        compiler_params=pltpu.CompilerParams(vmem_limit_bytes=32 * 1024 * 1024),
        cost_estimate=pl.CostEstimate(
            flops=2 * groups * mine * depth * columns, bytes_accessed=4 * 1024 * 1024, transcendentals=0
        ),
    )(place, *arrays)


def shards(attention, output_projection, residual, gain, draft_weight, down, up, tenant_of, tenant_count):
    n_z, n_yh, n_yl, n_x, _ = SIZES
    n_chips = n_yl * n_x
    tenants = tenant_count.shape[0]
    rank = down.shape[1]
    tokens, block = residual.shape
    cols = output_projection.shape[1]
    out_block = draft_weight.shape[1]
    width = block * 2 * n_chips
    mine = tokens // 2
    core = lax.axis_index("c")
    chip = lax.axis_index(CHIPS)
    other = 1 - core
    first = core == 0

    yh = lax.axis_index("yh")
    turned = (yh - jnp.arange(n_yh, dtype=jnp.int32)) % n_yh

    def around(value):
        return [value] + [
            lax.ppermute(value, "yh", [(i, (i + s) % n_yh) for i in range(n_yh)]) for s in range(1, n_yh)
        ]

    def ordered(own, others):
        return jnp.where(first, own, others), jnp.where(first, others, own)

    upper = jnp.concatenate([up.T, jnp.zeros((rank, block - out_block), BF)], axis=1)
    joined = gather(jnp.concatenate([attention, down.T, upper], axis=0), "z", n_z)
    pieces = around(output_projection)
    draft_weight_other = swap(draft_weight)
    pad = jnp.broadcast_to(gain[None], (16, block))
    kept = swap(jnp.concatenate([half(residual, other, mine), pad], axis=0))
    chip_rows = jnp.concatenate(
        ordered(jnp.concatenate([half(residual, core, mine), pad], axis=0), kept), axis=1
    )
    places = [(i, k) for i in range(n_z) for k in range(n_chips)]
    homes = [(i * n_chips + k, (i + k) % n_z * n_chips + k) for i, k in places]
    chips = [(i * n_chips + k, i * n_chips + (i - k) % n_chips) for i, k in places]
    chip_rows = lax.ppermute(chip_rows, ("z", "yl", "x"), chips)
    slot = jnp.arange(tenants * rank, dtype=jnp.int32) // rank
    slot_tenant = (slot % n_z) * n_yh + slot // n_z
    own_tenant = half(tenant_of, core, mine)
    partner_tenant = half(tenant_of, other, mine)
    own_mask = slot_tenant[:, None] == own_tenant[None, :]
    partner_mask = slot_tenant[:, None] == partner_tenant[None, :]
    following = jnp.roll(tenant_of, -1)
    position = jnp.arange(tokens, dtype=jnp.int32)
    keep_mask = (position < tokens - 1) & (tenant_of == following)
    is_tenant = tenant_of[:, None] == jnp.arange(tenants, dtype=jnp.int32)[None, :]
    count = jnp.sum(jnp.where(is_tenant, tenant_count.astype(F32)[None, :], 0.0), axis=1)
    weights = keep_mask.astype(F32) / count
    joined, chip_rows, own_mask, partner_mask, weights = lax.optimization_barrier(
        (joined, chip_rows, own_mask, partner_mask, weights)
    )
    residual_part, gain_part = chip_rows[:mine].astype(F32), chip_rows[mine : mine + 1].astype(F32)

    z = lax.axis_index("z")
    sent = swap(product(mine, other, z, joined, pieces))
    pair = product(mine, core, z, joined, pieces, sent)
    adapters = jnp.concatenate(
        [joined[:, tokens : tokens + rank], joined[:, tokens + rank :, :out_block]], axis=2
    ).reshape(n_z * rank, block + out_block)
    pair, adapters = lax.optimization_barrier((pair, adapters))
    parts = around(adapters)

    summed = jnp.sum(exchange(pair, CHIPS).astype(F32), axis=0).astype(BF)
    summed = jnp.stack([summed[:, s * cols : (s + 1) * cols] for s in range(n_yh)])
    projected = lax.ppermute(summed[turned], ("z", "yl", "x"), homes)

    hidden = residual_part + jnp.concatenate([projected[j] for j in range(n_yh)], axis=1).astype(F32)
    squares = jnp.sum(hidden * hidden, axis=1, keepdims=True)
    scaled = (hidden * gain_part).astype(BF)
    message = jnp.concatenate([scaled, *split(squares), jnp.zeros((mine, 126), BF)], axis=1)
    received = gather(message, CHIPS, n_chips)
    blocks = (z - jnp.arange(n_chips, dtype=jnp.int32)) % n_chips
    features = received[:, :, : 2 * block][blocks]
    totals = jnp.sum(received[:, :, 2 * block :].astype(F32), axis=0)
    inv_column = lax.rsqrt((totals[:, :1] + totals[:, 1:2]) / width + EPSILON)
    inv_row = jnp.broadcast_to(inv_column, (mine, 128)).T[:1]

    _, later = lax.optimization_barrier((message, turned))
    adapters_all = jnp.stack(parts)[later].reshape(tenants * rank, block + out_block)
    downs, ups = adapters_all[:, :block], adapters_all[:, block:]

    def select(values, mask):
        chosen = jnp.where(mask, values, 0.0)
        return jnp.sum(chosen.reshape(tenants, rank, mine), axis=0)

    def widen(values, mask):
        return jnp.where(mask, jnp.tile(values, (tenants, 1)), BF(0))

    chip_features = lax.dynamic_index_in_dim(features, chip, 0, keepdims=False)
    own_scaled = half(chip_features, core, block, 1)
    target = lax.dynamic_slice(
        features, (chip // 2, 0, (chip % 2) * 2 * out_block), (1, mine, 2 * out_block)
    )[0]
    target = (target.astype(F32) * inv_column).astype(BF)
    came = swap(jnp.concatenate([half(chip_features, other, block, 1), target[:16]], axis=0))
    partner_scaled, next_row = came[:mine], came[mine : mine + 1]
    low_parts = ordered(
        select(dot("jd,td->jt", downs, own_scaled), own_mask),
        select(dot("jd,td->jt", downs, partner_scaled), partner_mask),
    )
    target = jnp.concatenate([target[1:], next_row], axis=0)
    target = jnp.concatenate([half(target, core, out_block, 1), half(target, other, out_block, 1)], axis=1)

    weight, weight_row = half(weights, core, mine)[:, None], half(weights, core, mine)[None]
    partner_weight, partner_weight_row = half(weights, other, mine)[:, None], half(weights, other, mine)[None]

    def plain(columns, part):
        draft = dot("ktd,kdn->tn", features, columns.reshape(n_chips, 2 * block, out_block))
        return (draft * inv_column - target[:, part * out_block : (part + 1) * out_block].astype(F32)) * weight

    plain_other = plain(draft_weight_other, 1).astype(BF)
    lanes = jnp.concatenate([*split(inv_column), jnp.zeros((mine, 126), BF)], axis=1)
    partner = swap(jnp.concatenate([plain_other, lanes], axis=1))
    plain_own = plain(draft_weight, 0)

    back_parts = ordered(
        select(dot("jc,tc->jt", ups, plain_own.astype(BF)), own_mask),
        select(dot("jc,tc->jt", ups, partner[:, :out_block]), partner_mask),
    )
    square = jnp.where(slot[:, None] == slot[None, :], dot("jc,ic->ji", ups, ups), 0.0)
    square = jnp.sum(square.reshape(tenants, rank, tenants * rank), axis=0)
    codes = jnp.concatenate([*low_parts, *back_parts, square], axis=1).astype(BF)
    codes = jnp.sum(gather(codes, MP, 2 * n_chips).astype(F32), axis=0)
    square = codes[:, 4 * mine :].astype(BF)
    lows = ordered(codes[:, :mine], codes[:, mine : 2 * mine])
    backs = ordered(codes[:, 2 * mine : 3 * mine], codes[:, 3 * mine : 4 * mine])
    partner_inv = partner[:, out_block:].T
    partner_inv = partner_inv[:1].astype(F32) + partner_inv[1:2].astype(F32)

    def finish(low, back, mask, plain_grad, column, row, inv):
        low_wide = widen((low * inv).astype(BF), mask)
        term = ADAPTER_SCALE * dot("jt,jn->tn", low_wide, ups)
        grad = (plain_grad + term * column).astype(BF)
        back = back + ADAPTER_SCALE * dot("rj,jt->rt", square, low_wide) * row
        return low_wide, grad, widen((ADAPTER_SCALE * back * inv).astype(BF), mask)

    low_wide, grad, back_wide = finish(
        lows[0], backs[0], own_mask, plain_own, weight, weight_row, inv_row
    )
    partner_low, partner_grad, partner_back = finish(
        lows[1],
        backs[1],
        partner_mask,
        partner[:, :out_block].astype(F32),
        partner_weight,
        partner_weight_row,
        partner_inv,
    )
    grad_up = dot("jt,tc->jc", low_wide, grad) + dot("jt,tc->jc", partner_low, partner_grad)
    grad_down = dot("jt,td->jd", back_wide, own_scaled) + dot("jt,td->jd", partner_back, partner_scaled)
    grads = jnp.concatenate([grad_down.astype(BF), grad_up.astype(BF)], axis=1)
    grads = exchange(grads.reshape(tenants, rank, block + out_block), ("yh", "z"))
    grads = jnp.sum(grads.astype(F32), axis=0)
    return grads[:, :block].T, grads[:, block:].T


def solution(mesh):
    split_mesh = Mesh(mesh.devices.reshape(SIZES), AXES)
    return jax.shard_map(
        shards,
        mesh=split_mesh,
        in_specs=(
            P(DP, MP),
            P(MP, DP),
            P(DP, MP),
            P(MP),
            P(None, MP),
            P(MP, DP),
            P(MP, DP),
            P(DP),
            P(),
        ),
        out_specs=(P(MP, DP), P(MP, DP)),
        check_vma=False,
    )
```

```python
import functools

import jax
import jax.numpy as jnp
from jax import lax
from jax.experimental import pallas as pl
from jax.experimental.pallas import tpu as pltpu
from jax.sharding import Mesh
from jax.sharding import PartitionSpec as P

EPSILON = 1e-06
ADAPTER_SCALE = 2.0
BF = jnp.bfloat16
F32 = jnp.float32

AXES = ("z", "yh", "yl", "x", "c")
SIZES = (8, 4, 2, 4, 2)
DP = ("z", "yh")
MP = ("yl", "x", "c")
CHIPS = ("yl", "x")


def dot(subscripts, left, right):
    return jnp.einsum(subscripts, left, right, preferred_element_type=F32)


def swap(value):
    return lax.ppermute(value, "c", [(0, 1), (1, 0)])


def exchange(value, axis):
    return lax.all_to_all(value, axis, 0, 0)


def gather(value, axis, size):
    return exchange(jnp.broadcast_to(value[None], (size,) + value.shape), axis)


def split(value):
    high = value.astype(BF)
    return high, (value - high.astype(F32)).astype(BF)


def half(value, which, length, axis=0):
    return lax.dynamic_slice_in_dim(value, which * length, length, axis)


def product_kernel(mine, place, joined, *refs):
    *pieces, out, rows = refs
    came = pieces.pop() if len(pieces) > 4 else None
    groups = joined.shape[0]
    start = pl.multiple_of(place[0] * mine, mine)
    for k in range(groups):
        rows[pl.ds(k * mine, mine), :] = joined[(place[1] + k) % groups, pl.ds(start, mine), :]
    cols = pieces[0].shape[1]
    for s, piece in enumerate(pieces):
        total = jnp.dot(rows[...], piece[...], preferred_element_type=F32)
        total = total.reshape(groups, mine, cols)
        lanes = pl.ds(s * cols, cols)
        if came is not None:
            total = total + came[:, :, lanes].astype(F32)
        out[:, :, lanes] = total.astype(BF)


def product(mine, which, z, joined, pieces, came=None):
    groups, depth = joined.shape[0], joined.shape[2]
    columns = sum(piece.shape[1] for piece in pieces)
    place = jnp.stack([which, z]).astype(jnp.int32)
    arrays = [joined, *pieces] + ([] if came is None else [came])
    vmem = pl.BlockSpec(memory_space=pltpu.VMEM)
    return pl.pallas_call(
        functools.partial(product_kernel, mine),
        out_shape=jax.ShapeDtypeStruct((groups, mine, columns), BF),
        in_specs=[pl.BlockSpec(memory_space=pltpu.SMEM)] + [vmem] * len(arrays),
        out_specs=vmem,
        scratch_shapes=[pltpu.VMEM((groups * mine, depth), BF)],
        compiler_params=pltpu.CompilerParams(vmem_limit_bytes=32 * 1024 * 1024),
        cost_estimate=pl.CostEstimate(
            flops=2 * groups * mine * depth * columns, bytes_accessed=4 * 1024 * 1024, transcendentals=0
        ),
    )(place, *arrays)


def shards(attention, output_projection, residual, gain, draft_weight, down, up, tenant_of, tenant_count):
    n_z, n_yh, n_yl, n_x, _ = SIZES
    n_chips = n_yl * n_x
    tenants = tenant_count.shape[0]
    rank = down.shape[1]
    tokens, block = residual.shape
    cols = output_projection.shape[1]
    out_block = draft_weight.shape[1]
    width = block * 2 * n_chips
    mine = tokens // 2
    core = lax.axis_index("c")
    chip = lax.axis_index(CHIPS)
    other = 1 - core
    first = core == 0

    yh = lax.axis_index("yh")
    turned = (yh - jnp.arange(n_yh, dtype=jnp.int32)) % n_yh

    def shift(value, step):
        return lax.ppermute(value, "yh", [(i, (i + step) % n_yh) for i in range(n_yh)])

    def ordered(own, others):
        return jnp.where(first, own, others), jnp.where(first, others, own)

    upper = jnp.concatenate([up.T, jnp.zeros((rank, block - out_block), BF)], axis=1)
    joined = gather(jnp.concatenate([attention, down.T, upper], axis=0), "z", n_z)
    pieces = [output_projection] + [shift(output_projection, step) for step in range(1, n_yh)]
    draft_weight_other = swap(draft_weight)
    pad = jnp.broadcast_to(gain[None], (16, block))
    kept = swap(jnp.concatenate([half(residual, other, mine), pad], axis=0))
    chip_rows = jnp.concatenate(
        ordered(jnp.concatenate([half(residual, core, mine), pad], axis=0), kept), axis=1
    )
    places = [(i, k) for i in range(n_z) for k in range(n_chips)]
    homes = [(i * n_chips + k, (i + k) % n_z * n_chips + k) for i, k in places]
    chips = [(i * n_chips + k, i * n_chips + (i - k) % n_chips) for i, k in places]
    chip_rows = lax.ppermute(chip_rows, ("z", "yl", "x"), chips)
    slot = jnp.arange(tenants * rank, dtype=jnp.int32) // rank
    slot_tenant = (slot % n_z) * n_yh + slot // n_z
    own_tenant = half(tenant_of, core, mine)
    partner_tenant = half(tenant_of, other, mine)
    own_mask = slot_tenant[:, None] == own_tenant[None, :]
    partner_mask = slot_tenant[:, None] == partner_tenant[None, :]
    following = jnp.roll(tenant_of, -1)
    position = jnp.arange(tokens, dtype=jnp.int32)
    keep_mask = (position < tokens - 1) & (tenant_of == following)
    is_tenant = tenant_of[:, None] == jnp.arange(tenants, dtype=jnp.int32)[None, :]
    count = jnp.sum(jnp.where(is_tenant, tenant_count.astype(F32)[None, :], 0.0), axis=1)
    weights = keep_mask.astype(F32) / count
    joined, chip_rows, own_mask, partner_mask, weights = lax.optimization_barrier(
        (joined, chip_rows, own_mask, partner_mask, weights)
    )
    residual_part, gain_part = chip_rows[:mine].astype(F32), chip_rows[mine : mine + 1].astype(F32)

    z = lax.axis_index("z")
    sent = swap(product(mine, other, z, joined, pieces))
    pair = product(mine, core, z, joined, pieces, sent)
    adapters = jnp.concatenate(
        [joined[:, tokens : tokens + rank], joined[:, tokens + rank :, :out_block]], axis=2
    ).reshape(n_z * rank, block + out_block)
    pair, adapters = lax.optimization_barrier((pair, adapters))
    before, after = shift(adapters, 1), shift(adapters, -1)

    summed = jnp.sum(exchange(pair, CHIPS).astype(F32), axis=0).astype(BF)
    summed = jnp.stack([summed[:, s * cols : (s + 1) * cols] for s in range(n_yh)])
    projected = lax.ppermute(summed[turned], ("z", "yl", "x"), homes)

    projected, before, after = lax.optimization_barrier((projected, before, after))
    some = n_z * rank // 2
    far = jnp.concatenate([shift(before[:some], 1), shift(after[some:], -1)], axis=0)
    parts = [adapters, before, far, after]

    hidden = residual_part + jnp.concatenate([projected[j] for j in range(n_yh)], axis=1).astype(F32)
    squares = jnp.sum(hidden * hidden, axis=1, keepdims=True)
    scaled = (hidden * gain_part).astype(BF)
    message = jnp.concatenate([scaled, *split(squares), jnp.zeros((mine, 126), BF)], axis=1)
    received = gather(message, CHIPS, n_chips)
    blocks = (z - jnp.arange(n_chips, dtype=jnp.int32)) % n_chips
    features = received[:, :, : 2 * block][blocks]
    totals = jnp.sum(received[:, :, 2 * block :].astype(F32), axis=0)
    inv_column = lax.rsqrt((totals[:, :1] + totals[:, 1:2]) / width + EPSILON)
    inv_row = jnp.broadcast_to(inv_column, (mine, 128)).T[:1]

    _, later = lax.optimization_barrier((message, turned))
    adapters_all = jnp.stack(parts)[later].reshape(tenants * rank, block + out_block)
    downs, ups = adapters_all[:, :block], adapters_all[:, block:]

    def select(values, mask):
        chosen = jnp.where(mask, values, 0.0)
        return jnp.sum(chosen.reshape(tenants, rank, mine), axis=0)

    def widen(values, mask):
        return jnp.where(mask, jnp.tile(values, (tenants, 1)), BF(0))

    chip_features = lax.dynamic_index_in_dim(features, chip, 0, keepdims=False)
    own_scaled = half(chip_features, core, block, 1)
    target = lax.dynamic_slice(
        features, (chip // 2, 0, (chip % 2) * 2 * out_block), (1, mine, 2 * out_block)
    )[0]
    target = (target.astype(F32) * inv_column).astype(BF)
    came = swap(jnp.concatenate([half(chip_features, other, block, 1), target[:16]], axis=0))
    partner_scaled, next_row = came[:mine], came[mine : mine + 1]
    low_parts = ordered(
        select(dot("jd,td->jt", downs, own_scaled), own_mask),
        select(dot("jd,td->jt", downs, partner_scaled), partner_mask),
    )
    target = jnp.concatenate([target[1:], next_row], axis=0)
    target = jnp.concatenate([half(target, core, out_block, 1), half(target, other, out_block, 1)], axis=1)

    weight, weight_row = half(weights, core, mine)[:, None], half(weights, core, mine)[None]
    partner_weight, partner_weight_row = half(weights, other, mine)[:, None], half(weights, other, mine)[None]

    def plain(columns, part):
        draft = dot("ktd,kdn->tn", features, columns.reshape(n_chips, 2 * block, out_block))
        return (draft * inv_column - target[:, part * out_block : (part + 1) * out_block].astype(F32)) * weight

    plain_other = plain(draft_weight_other, 1).astype(BF)
    lanes = jnp.concatenate([*split(inv_column), jnp.zeros((mine, 126), BF)], axis=1)
    partner = swap(jnp.concatenate([plain_other, lanes], axis=1))
    plain_own = plain(draft_weight, 0)

    back_parts = ordered(
        select(dot("jc,tc->jt", ups, plain_own.astype(BF)), own_mask),
        select(dot("jc,tc->jt", ups, partner[:, :out_block]), partner_mask),
    )
    square = jnp.where(slot[:, None] == slot[None, :], dot("jc,ic->ji", ups, ups), 0.0)
    square = jnp.sum(square.reshape(tenants, rank, tenants * rank), axis=0)
    codes = jnp.concatenate([*low_parts, *back_parts, square], axis=1).astype(BF)
    codes = jnp.sum(gather(codes, MP, 2 * n_chips).astype(F32), axis=0)
    square = codes[:, 4 * mine :].astype(BF)
    lows = ordered(codes[:, :mine], codes[:, mine : 2 * mine])
    backs = ordered(codes[:, 2 * mine : 3 * mine], codes[:, 3 * mine : 4 * mine])
    partner_inv = partner[:, out_block:].T
    partner_inv = partner_inv[:1].astype(F32) + partner_inv[1:2].astype(F32)

    def finish(low, back, mask, plain_grad, column, row, inv):
        low_wide = widen((low * inv).astype(BF), mask)
        term = ADAPTER_SCALE * dot("jt,jn->tn", low_wide, ups)
        grad = (plain_grad + term * column).astype(BF)
        back = back + ADAPTER_SCALE * dot("rj,jt->rt", square, low_wide) * row
        return low_wide, grad, widen((ADAPTER_SCALE * back * inv).astype(BF), mask)

    low_wide, grad, back_wide = finish(
        lows[0], backs[0], own_mask, plain_own, weight, weight_row, inv_row
    )
    partner_low, partner_grad, partner_back = finish(
        lows[1],
        backs[1],
        partner_mask,
        partner[:, :out_block].astype(F32),
        partner_weight,
        partner_weight_row,
        partner_inv,
    )
    grad_up = dot("jt,tc->jc", low_wide, grad) + dot("jt,tc->jc", partner_low, partner_grad)
    grad_down = dot("jt,td->jd", back_wide, own_scaled) + dot("jt,td->jd", partner_back, partner_scaled)
    grads = jnp.concatenate([grad_down.astype(BF), grad_up.astype(BF)], axis=1)
    grads = exchange(grads.reshape(tenants, rank, block + out_block), ("yh", "z"))
    grads = jnp.sum(grads.astype(F32), axis=0)
    return grads[:, :block].T, grads[:, block:].T


def solution(mesh):
    split_mesh = Mesh(mesh.devices.reshape(SIZES), AXES)
    return jax.shard_map(
        shards,
        mesh=split_mesh,
        in_specs=(
            P(DP, MP),
            P(MP, DP),
            P(DP, MP),
            P(MP),
            P(None, MP),
            P(MP, DP),
            P(MP, DP),
            P(DP),
            P(),
        ),
        out_specs=(P(MP, DP), P(MP, DP)),
        check_vma=False,
    )
```

```python
import functools

import jax
import jax.numpy as jnp
from jax import lax
from jax.experimental import pallas as pl
from jax.experimental.pallas import tpu as pltpu
from jax.sharding import Mesh
from jax.sharding import PartitionSpec as P

EPSILON = 1e-06
ADAPTER_SCALE = 2.0
BF = jnp.bfloat16
F32 = jnp.float32

AXES = ("z", "yh", "yl", "x", "c")
SIZES = (8, 4, 2, 4, 2)
DP = ("z", "yh")
MP = ("yl", "x", "c")
CHIPS = ("yl", "x")


def dot(subscripts, left, right):
    return jnp.einsum(subscripts, left, right, preferred_element_type=F32)


def swap(value):
    return lax.ppermute(value, "c", [(0, 1), (1, 0)])


def exchange(value, axis):
    return lax.all_to_all(value, axis, 0, 0)


def gather(value, axis, size):
    return exchange(jnp.broadcast_to(value[None], (size,) + value.shape), axis)


def split(value):
    high = value.astype(BF)
    return high, (value - high.astype(F32)).astype(BF)


def half(value, which, length, axis=0):
    return lax.dynamic_slice_in_dim(value, which * length, length, axis)


def product_kernel(mine, place, joined, *refs):
    *pieces, out, rows = refs
    came = pieces.pop() if len(pieces) > 4 else None
    groups = joined.shape[0]
    start = pl.multiple_of(place[0] * mine, mine)
    for k in range(groups):
        rows[pl.ds(k * mine, mine), :] = joined[(place[1] + k) % groups, pl.ds(start, mine), :]
    cols = pieces[0].shape[1]
    for s, piece in enumerate(pieces):
        total = jnp.dot(rows[...], piece[...], preferred_element_type=F32)
        total = total.reshape(groups, mine, cols)
        lanes = pl.ds(s * cols, cols)
        if came is not None:
            total = total + came[:, :, lanes].astype(F32)
        out[:, :, lanes] = total.astype(BF)


def product(mine, which, z, joined, pieces, came=None):
    groups, depth = joined.shape[0], joined.shape[2]
    columns = sum(piece.shape[1] for piece in pieces)
    place = jnp.stack([which, z]).astype(jnp.int32)
    arrays = [joined, *pieces] + ([] if came is None else [came])
    vmem = pl.BlockSpec(memory_space=pltpu.VMEM)
    return pl.pallas_call(
        functools.partial(product_kernel, mine),
        out_shape=jax.ShapeDtypeStruct((groups, mine, columns), BF),
        in_specs=[pl.BlockSpec(memory_space=pltpu.SMEM)] + [vmem] * len(arrays),
        out_specs=vmem,
        scratch_shapes=[pltpu.VMEM((groups * mine, depth), BF)],
        compiler_params=pltpu.CompilerParams(vmem_limit_bytes=32 * 1024 * 1024),
        cost_estimate=pl.CostEstimate(
            flops=2 * groups * mine * depth * columns, bytes_accessed=4 * 1024 * 1024, transcendentals=0
        ),
    )(place, *arrays)


def shards(attention, output_projection, residual, gain, draft_weight, down, up, tenant_of, tenant_count):
    n_z, n_yh, n_yl, n_x, _ = SIZES
    n_chips = n_yl * n_x
    tenants = tenant_count.shape[0]
    rank = down.shape[1]
    tokens, block = residual.shape
    cols = output_projection.shape[1]
    out_block = draft_weight.shape[1]
    width = block * 2 * n_chips
    mine = tokens // 2
    core = lax.axis_index("c")
    chip = lax.axis_index(CHIPS)
    other = 1 - core
    first = core == 0

    yh = lax.axis_index("yh")
    turned = (yh - jnp.arange(n_yh, dtype=jnp.int32)) % n_yh

    def around(value):
        return [value] + [
            lax.ppermute(value, "yh", [(i, (i + s) % n_yh) for i in range(n_yh)]) for s in range(1, n_yh)
        ]

    def ordered(own, others):
        return jnp.where(first, own, others), jnp.where(first, others, own)

    upper = jnp.concatenate([up.T, jnp.zeros((rank, block - out_block), BF)], axis=1)
    joined = gather(jnp.concatenate([attention, down.T, upper], axis=0), "z", n_z)
    pieces = around(output_projection)
    draft_weight_other = swap(draft_weight)
    pad = jnp.broadcast_to(gain[None], (16, block))
    kept = swap(jnp.concatenate([half(residual, other, mine), pad], axis=0))
    chip_rows = jnp.concatenate(
        ordered(jnp.concatenate([half(residual, core, mine), pad], axis=0), kept), axis=1
    )
    places = [(i, k) for i in range(n_z) for k in range(n_chips)]
    homes = [(i * n_chips + k, (i + k) % n_z * n_chips + k) for i, k in places]
    chips = [(i * n_chips + k, i * n_chips + (i - k) % n_chips) for i, k in places]
    chip_rows = lax.ppermute(chip_rows, ("z", "yl", "x"), chips)
    slot = jnp.arange(tenants * rank, dtype=jnp.int32) // rank
    slot_tenant = (slot % n_z) * n_yh + slot // n_z
    own_tenant = half(tenant_of, core, mine)
    partner_tenant = half(tenant_of, other, mine)
    own_mask = slot_tenant[:, None] == own_tenant[None, :]
    partner_mask = slot_tenant[:, None] == partner_tenant[None, :]
    following = jnp.roll(tenant_of, -1)
    position = jnp.arange(tokens, dtype=jnp.int32)
    keep_mask = (position < tokens - 1) & (tenant_of == following)
    is_tenant = tenant_of[:, None] == jnp.arange(tenants, dtype=jnp.int32)[None, :]
    count = jnp.sum(jnp.where(is_tenant, tenant_count.astype(F32)[None, :], 0.0), axis=1)
    weights = keep_mask.astype(F32) / count
    joined, chip_rows, own_mask, partner_mask, weights = lax.optimization_barrier(
        (joined, chip_rows, own_mask, partner_mask, weights)
    )
    residual_part, gain_part = chip_rows[:mine].astype(F32), chip_rows[mine : mine + 1].astype(F32)

    z = lax.axis_index("z")
    sent = swap(product(mine, other, z, joined, pieces))
    pair = product(mine, core, z, joined, pieces, sent)
    adapters = jnp.concatenate(
        [joined[:, tokens : tokens + rank], joined[:, tokens + rank :, :out_block]], axis=2
    ).reshape(n_z * rank, block + out_block)
    pair, adapters = lax.optimization_barrier((pair, adapters))
    parts = around(adapters)

    summed = jnp.sum(exchange(pair, CHIPS).astype(F32), axis=0).astype(BF)
    summed = jnp.stack([summed[:, s * cols : (s + 1) * cols] for s in range(n_yh)])
    projected = lax.ppermute(summed[turned], ("z", "yl", "x"), homes)
    projected, *parts = lax.optimization_barrier((projected, *parts))

    hidden = residual_part + jnp.concatenate([projected[j] for j in range(n_yh)], axis=1).astype(F32)
    squares = jnp.sum(hidden * hidden, axis=1, keepdims=True)
    scaled = (hidden * gain_part).astype(BF)
    message = jnp.concatenate([scaled, *split(squares), jnp.zeros((mine, 126), BF)], axis=1)
    received = gather(message, CHIPS, n_chips)
    blocks = (z - jnp.arange(n_chips, dtype=jnp.int32)) % n_chips
    features = received[:, :, : 2 * block][blocks]
    totals = jnp.sum(received[:, :, 2 * block :].astype(F32), axis=0)
    inv_column = lax.rsqrt((totals[:, :1] + totals[:, 1:2]) / width + EPSILON)
    inv_row = jnp.broadcast_to(inv_column, (mine, 128)).T[:1]

    adapters_all = jnp.stack(parts)[turned].reshape(tenants * rank, block + out_block)
    downs, ups = adapters_all[:, :block], adapters_all[:, block:]

    def select(values, mask):
        chosen = jnp.where(mask, values, 0.0)
        return jnp.sum(chosen.reshape(tenants, rank, mine), axis=0)

    def widen(values, mask):
        return jnp.where(mask, jnp.tile(values, (tenants, 1)), BF(0))

    chip_features = lax.dynamic_index_in_dim(features, chip, 0, keepdims=False)
    own_scaled = half(chip_features, core, block, 1)
    target = lax.dynamic_slice(
        features, (chip // 2, 0, (chip % 2) * 2 * out_block), (1, mine, 2 * out_block)
    )[0]
    target = (target.astype(F32) * inv_column).astype(BF)
    came = swap(jnp.concatenate([half(chip_features, other, block, 1), target[:16]], axis=0))
    partner_scaled, next_row = came[:mine], came[mine : mine + 1]
    low_parts = ordered(
        select(dot("jd,td->jt", downs, own_scaled), own_mask),
        select(dot("jd,td->jt", downs, partner_scaled), partner_mask),
    )
    target = jnp.concatenate([target[1:], next_row], axis=0)
    target = jnp.concatenate([half(target, core, out_block, 1), half(target, other, out_block, 1)], axis=1)

    weight, weight_row = half(weights, core, mine)[:, None], half(weights, core, mine)[None]
    partner_weight, partner_weight_row = half(weights, other, mine)[:, None], half(weights, other, mine)[None]

    def plain(columns, part):
        draft = dot("ktd,kdn->tn", features, columns.reshape(n_chips, 2 * block, out_block))
        return (draft * inv_column - target[:, part * out_block : (part + 1) * out_block].astype(F32)) * weight

    plain_other = plain(draft_weight_other, 1).astype(BF)
    lanes = jnp.concatenate([*split(inv_column), jnp.zeros((mine, 126), BF)], axis=1)
    partner = swap(jnp.concatenate([plain_other, lanes], axis=1))
    plain_own = plain(draft_weight, 0)

    back_parts = ordered(
        select(dot("jc,tc->jt", ups, plain_own.astype(BF)), own_mask),
        select(dot("jc,tc->jt", ups, partner[:, :out_block]), partner_mask),
    )
    square = jnp.where(slot[:, None] == slot[None, :], dot("jc,ic->ji", ups, ups), 0.0)
    square = jnp.sum(square.reshape(tenants, rank, tenants * rank), axis=0)
    codes = jnp.concatenate([*low_parts, *back_parts, square], axis=1).astype(BF)
    codes = jnp.sum(gather(codes, MP, 2 * n_chips).astype(F32), axis=0)
    square = codes[:, 4 * mine :].astype(BF)
    lows = ordered(codes[:, :mine], codes[:, mine : 2 * mine])
    backs = ordered(codes[:, 2 * mine : 3 * mine], codes[:, 3 * mine : 4 * mine])
    partner_inv = partner[:, out_block:].T
    partner_inv = partner_inv[:1].astype(F32) + partner_inv[1:2].astype(F32)

    def finish(low, back, mask, plain_grad, column, row, inv):
        low_wide = widen((low * inv).astype(BF), mask)
        term = ADAPTER_SCALE * dot("jt,jn->tn", low_wide, ups)
        grad = (plain_grad + term * column).astype(BF)
        back = back + ADAPTER_SCALE * dot("rj,jt->rt", square, low_wide) * row
        return low_wide, grad, widen((ADAPTER_SCALE * back * inv).astype(BF), mask)

    low_wide, grad, back_wide = finish(
        lows[0], backs[0], own_mask, plain_own, weight, weight_row, inv_row
    )
    partner_low, partner_grad, partner_back = finish(
        lows[1],
        backs[1],
        partner_mask,
        partner[:, :out_block].astype(F32),
        partner_weight,
        partner_weight_row,
        partner_inv,
    )
    grad_up = dot("jt,tc->jc", low_wide, grad) + dot("jt,tc->jc", partner_low, partner_grad)
    grad_down = dot("jt,td->jd", back_wide, own_scaled) + dot("jt,td->jd", partner_back, partner_scaled)
    grads = jnp.concatenate([grad_down.astype(BF), grad_up.astype(BF)], axis=1)
    grads = exchange(grads.reshape(tenants, rank, block + out_block), ("yh", "z"))
    grads = jnp.sum(grads.astype(F32), axis=0)
    return grads[:, :block].T, grads[:, block:].T


def solution(mesh):
    split_mesh = Mesh(mesh.devices.reshape(SIZES), AXES)
    return jax.shard_map(
        shards,
        mesh=split_mesh,
        in_specs=(
            P(DP, MP),
            P(MP, DP),
            P(DP, MP),
            P(MP),
            P(None, MP),
            P(MP, DP),
            P(MP, DP),
            P(DP),
            P(),
        ),
        out_specs=(P(MP, DP), P(MP, DP)),
        check_vma=False,
    )
```

```python
import functools

import jax
import jax.numpy as jnp
from jax import lax
from jax.experimental import pallas as pl
from jax.experimental.pallas import tpu as pltpu
from jax.sharding import Mesh
from jax.sharding import PartitionSpec as P

EPSILON = 1e-06
ADAPTER_SCALE = 2.0
BF = jnp.bfloat16
F32 = jnp.float32

AXES = ("z", "yh", "yl", "x", "c")
SIZES = (8, 4, 2, 4, 2)
DP = ("z", "yh")
MP = ("yl", "x", "c")
CHIPS = ("yl", "x")


def dot(subscripts, left, right):
    return jnp.einsum(subscripts, left, right, preferred_element_type=F32)


def swap(value):
    return lax.ppermute(value, "c", [(0, 1), (1, 0)])


def exchange(value, axis):
    return lax.all_to_all(value, axis, 0, 0)


def gather(value, axis, size):
    return exchange(jnp.broadcast_to(value[None], (size,) + value.shape), axis)


def split(value):
    high = value.astype(BF)
    return high, (value - high.astype(F32)).astype(BF)


def half(value, which, length, axis=0):
    return lax.dynamic_slice_in_dim(value, which * length, length, axis)


def product_kernel(mine, place, joined, *refs):
    *pieces, out, rows = refs
    came = pieces.pop() if len(pieces) > 4 else None
    groups = joined.shape[0]
    start = pl.multiple_of(place[0] * mine, mine)
    for k in range(groups):
        rows[pl.ds(k * mine, mine), :] = joined[(place[1] + k) % groups, pl.ds(start, mine), :]
    cols = pieces[0].shape[1]
    for s, piece in enumerate(pieces):
        total = jnp.dot(rows[...], piece[...], preferred_element_type=F32)
        total = total.reshape(groups, mine, cols)
        lanes = pl.ds(s * cols, cols)
        if came is not None:
            total = total + came[:, :, lanes].astype(F32)
        out[:, :, lanes] = total.astype(BF)


def product(mine, which, z, joined, pieces, came=None):
    groups, depth = joined.shape[0], joined.shape[2]
    columns = sum(piece.shape[1] for piece in pieces)
    place = jnp.stack([which, z]).astype(jnp.int32)
    arrays = [joined, *pieces] + ([] if came is None else [came])
    vmem = pl.BlockSpec(memory_space=pltpu.VMEM)
    return pl.pallas_call(
        functools.partial(product_kernel, mine),
        out_shape=jax.ShapeDtypeStruct((groups, mine, columns), BF),
        in_specs=[pl.BlockSpec(memory_space=pltpu.SMEM)] + [vmem] * len(arrays),
        out_specs=vmem,
        scratch_shapes=[pltpu.VMEM((groups * mine, depth), BF)],
        compiler_params=pltpu.CompilerParams(vmem_limit_bytes=32 * 1024 * 1024),
        cost_estimate=pl.CostEstimate(
            flops=2 * groups * mine * depth * columns, bytes_accessed=4 * 1024 * 1024, transcendentals=0
        ),
    )(place, *arrays)


def shards(attention, output_projection, residual, gain, draft_weight, down, up, tenant_of, tenant_count):
    n_z, n_yh, n_yl, n_x, _ = SIZES
    n_chips = n_yl * n_x
    tenants = tenant_count.shape[0]
    rank = down.shape[1]
    tokens, block = residual.shape
    cols = output_projection.shape[1]
    out_block = draft_weight.shape[1]
    width = block * 2 * n_chips
    mine = tokens // 2
    core = lax.axis_index("c")
    chip = lax.axis_index(CHIPS)
    other = 1 - core
    first = core == 0

    yh = lax.axis_index("yh")
    turned = (yh - jnp.arange(n_yh, dtype=jnp.int32)) % n_yh

    def around(value):
        return [value] + [
            lax.ppermute(value, "yh", [(i, (i + s) % n_yh) for i in range(n_yh)]) for s in range(1, n_yh)
        ]

    def ordered(own, others):
        return jnp.where(first, own, others), jnp.where(first, others, own)

    upper = jnp.concatenate([up.T[: rank // 2], up.T[rank // 2 :]], axis=1)
    joined = gather(jnp.concatenate([attention, down.T, upper], axis=0), "z", n_z)
    pieces = around(output_projection)
    draft_weight_other = swap(draft_weight)
    pad = jnp.broadcast_to(gain[None], (16, block))
    kept = swap(jnp.concatenate([half(residual, other, mine), pad], axis=0))
    chip_rows = jnp.concatenate(
        ordered(jnp.concatenate([half(residual, core, mine), pad], axis=0), kept), axis=1
    )
    places = [(i, k) for i in range(n_z) for k in range(n_chips)]
    homes = [(i * n_chips + k, (i + k) % n_z * n_chips + k) for i, k in places]
    chips = [(i * n_chips + k, i * n_chips + (i - k) % n_chips) for i, k in places]
    chip_rows = lax.ppermute(chip_rows, ("z", "yl", "x"), chips)
    slot = jnp.arange(tenants * rank, dtype=jnp.int32) // rank
    slot_tenant = (slot % n_z) * n_yh + slot // n_z
    own_tenant = half(tenant_of, core, mine)
    partner_tenant = half(tenant_of, other, mine)
    own_mask = slot_tenant[:, None] == own_tenant[None, :]
    partner_mask = slot_tenant[:, None] == partner_tenant[None, :]
    following = jnp.roll(tenant_of, -1)
    position = jnp.arange(tokens, dtype=jnp.int32)
    keep_mask = (position < tokens - 1) & (tenant_of == following)
    is_tenant = tenant_of[:, None] == jnp.arange(tenants, dtype=jnp.int32)[None, :]
    count = jnp.sum(jnp.where(is_tenant, tenant_count.astype(F32)[None, :], 0.0), axis=1)
    weights = keep_mask.astype(F32) / count
    joined, chip_rows, own_mask, partner_mask, weights = lax.optimization_barrier(
        (joined, chip_rows, own_mask, partner_mask, weights)
    )
    residual_part, gain_part = chip_rows[:mine].astype(F32), chip_rows[mine : mine + 1].astype(F32)

    z = lax.axis_index("z")
    sent = swap(product(mine, other, z, joined, pieces))
    pair = product(mine, core, z, joined, pieces, sent)
    uppers = joined[:, tokens + rank :]
    uppers = jnp.concatenate([uppers[:, :, :out_block], uppers[:, :, out_block:]], axis=1)
    adapters = jnp.concatenate([joined[:, tokens : tokens + rank], uppers], axis=2).reshape(n_z * rank, block + out_block)
    pair, adapters = lax.optimization_barrier((pair, adapters))
    parts = around(adapters)

    summed = jnp.sum(exchange(pair, CHIPS).astype(F32), axis=0).astype(BF)
    summed = jnp.stack([summed[:, s * cols : (s + 1) * cols] for s in range(n_yh)])
    projected = lax.ppermute(summed[turned], ("z", "yl", "x"), homes)
    projected, *parts = lax.optimization_barrier((projected, *parts))

    hidden = residual_part + jnp.concatenate([projected[j] for j in range(n_yh)], axis=1).astype(F32)
    squares = jnp.sum(hidden * hidden, axis=1, keepdims=True)
    scaled = (hidden * gain_part).astype(BF)
    message = jnp.concatenate([scaled, *split(squares), jnp.zeros((mine, 126), BF)], axis=1)
    received = gather(message, CHIPS, n_chips)
    blocks = (z - jnp.arange(n_chips, dtype=jnp.int32)) % n_chips
    features = received[:, :, : 2 * block][blocks]
    totals = jnp.sum(received[:, :, 2 * block :].astype(F32), axis=0)
    inv_column = lax.rsqrt((totals[:, :1] + totals[:, 1:2]) / width + EPSILON)
    inv_row = jnp.broadcast_to(inv_column, (mine, 128)).T[:1]

    adapters_all = jnp.stack(parts)[turned].reshape(tenants * rank, block + out_block)
    downs, ups = adapters_all[:, :block], adapters_all[:, block:]

    def select(values, mask):
        chosen = jnp.where(mask, values, 0.0)
        return jnp.sum(chosen.reshape(tenants, rank, mine), axis=0)

    def widen(values, mask):
        return jnp.where(mask, jnp.tile(values, (tenants, 1)), BF(0))

    chip_features = lax.dynamic_index_in_dim(features, chip, 0, keepdims=False)
    own_scaled = half(chip_features, core, block, 1)
    target = lax.dynamic_slice(
        features, (chip // 2, 0, (chip % 2) * 2 * out_block), (1, mine, 2 * out_block)
    )[0]
    target = (target.astype(F32) * inv_column).astype(BF)
    came = swap(jnp.concatenate([half(chip_features, other, block, 1), target[:16]], axis=0))
    partner_scaled, next_row = came[:mine], came[mine : mine + 1]
    low_parts = ordered(
        select(dot("jd,td->jt", downs, own_scaled), own_mask),
        select(dot("jd,td->jt", downs, partner_scaled), partner_mask),
    )
    target = jnp.concatenate([target[1:], next_row], axis=0)
    target = jnp.concatenate([half(target, core, out_block, 1), half(target, other, out_block, 1)], axis=1)

    weight, weight_row = half(weights, core, mine)[:, None], half(weights, core, mine)[None]
    partner_weight, partner_weight_row = half(weights, other, mine)[:, None], half(weights, other, mine)[None]

    def plain(columns, part):
        draft = dot("ktd,kdn->tn", features, columns.reshape(n_chips, 2 * block, out_block))
        return (draft * inv_column - target[:, part * out_block : (part + 1) * out_block].astype(F32)) * weight

    plain_other = plain(draft_weight_other, 1).astype(BF)
    lanes = jnp.concatenate([*split(inv_column), jnp.zeros((mine, 126), BF)], axis=1)
    partner = swap(jnp.concatenate([plain_other, lanes], axis=1))
    plain_own = plain(draft_weight, 0)

    back_parts = ordered(
        select(dot("jc,tc->jt", ups, plain_own.astype(BF)), own_mask),
        select(dot("jc,tc->jt", ups, partner[:, :out_block]), partner_mask),
    )
    square = jnp.where(slot[:, None] == slot[None, :], dot("jc,ic->ji", ups, ups), 0.0)
    square = jnp.sum(square.reshape(tenants, rank, tenants * rank), axis=0)
    codes = jnp.concatenate([*low_parts, *back_parts, square], axis=1).astype(BF)
    codes = jnp.sum(gather(codes, MP, 2 * n_chips).astype(F32), axis=0)
    square = codes[:, 4 * mine :].astype(BF)
    lows = ordered(codes[:, :mine], codes[:, mine : 2 * mine])
    backs = ordered(codes[:, 2 * mine : 3 * mine], codes[:, 3 * mine : 4 * mine])
    partner_inv = partner[:, out_block:].T
    partner_inv = partner_inv[:1].astype(F32) + partner_inv[1:2].astype(F32)

    def finish(low, back, mask, plain_grad, column, row, inv):
        low_wide = widen((low * inv).astype(BF), mask)
        term = ADAPTER_SCALE * dot("jt,jn->tn", low_wide, ups)
        grad = (plain_grad + term * column).astype(BF)
        back = back + ADAPTER_SCALE * dot("rj,jt->rt", square, low_wide) * row
        return low_wide, grad, widen((ADAPTER_SCALE * back * inv).astype(BF), mask)

    low_wide, grad, back_wide = finish(
        lows[0], backs[0], own_mask, plain_own, weight, weight_row, inv_row
    )
    partner_low, partner_grad, partner_back = finish(
        lows[1],
        backs[1],
        partner_mask,
        partner[:, :out_block].astype(F32),
        partner_weight,
        partner_weight_row,
        partner_inv,
    )
    grad_up = dot("jt,tc->jc", low_wide, grad) + dot("jt,tc->jc", partner_low, partner_grad)
    grad_down = dot("jt,td->jd", back_wide, own_scaled) + dot("jt,td->jd", partner_back, partner_scaled)
    grads = jnp.concatenate([grad_down.astype(BF), grad_up.astype(BF)], axis=1)
    grads = exchange(grads.reshape(tenants, rank, block + out_block), ("yh", "z"))
    grads = jnp.sum(grads.astype(F32), axis=0)
    return grads[:, :block].T, grads[:, block:].T


def solution(mesh):
    split_mesh = Mesh(mesh.devices.reshape(SIZES), AXES)
    return jax.shard_map(
        shards,
        mesh=split_mesh,
        in_specs=(
            P(DP, MP),
            P(MP, DP),
            P(DP, MP),
            P(MP),
            P(None, MP),
            P(MP, DP),
            P(MP, DP),
            P(DP),
            P(),
        ),
        out_specs=(P(MP, DP), P(MP, DP)),
        check_vma=False,
    )
```
